32 devices in a mesh: dp: 16 (over z, y, core), tensor: 2 (over x).
Axes of the slice: x: 2, y: 2, z: 4, core: 2. Of those that a mesh axis runs over, the one named last changes fastest.
Arguments:
- char_ids: int32 [8192, 50], P(('dp', 'tensor')), may hold values from 0 to 261
- mask_pos: int32 [16, 76], P('dp'), may hold values from 0 to 511
- out_grad: float32 [16, 76, 768], P('dp'), may hold values from -6 to 6
- char_table: bfloat16 [262, 16], replicated, may hold values from -6 to 6
- conv_weight: bfloat16 [112, 2048], P(None, ('dp', 'tensor')), may hold values from -1.5 to 1.5
- conv_bias: bfloat16 [2048], P(('dp', 'tensor')), may hold values from -8 to -2
- highway_weight: bfloat16 [2, 2048, 2, 2048], P(None, None, None, ('dp', 'tensor')), may hold values from -0.125 to 0.125
- highway_bias: bfloat16 [2, 2, 2048], P(None, None, ('dp', 'tensor')), may hold values from -3 to 3
- proj_weight: bfloat16 [2048, 768], P(('dp', 'tensor')), may hold values from -0.0625 to 0.0625
- proj_bias: bfloat16 [768], replicated, may hold values from -2 to 2
- qkv_weight: bfloat16 [768, 3, 768], P(None, None, 'tensor'), may hold values from -0.21875 to 0.21875
- qv_bias: bfloat16 [2, 768], P(None, 'tensor'), may hold values from -2 to 2
- out_weight: bfloat16 [768, 768], P('tensor'), may hold values from -3 to 3
- out_bias: bfloat16 [768], replicated, may hold values from -2 to 2
- ln1_gain: bfloat16 [768], replicated, may hold values from 0.25 to 1.75
- ln1_bias: bfloat16 [768], replicated, may hold values from -2 to 2
- up_weight: bfloat16 [768, 3072], P(None, 'tensor'), may hold values from -0.21875 to 0.21875
- up_bias: bfloat16 [3072], P('tensor'), may hold values from -2 to 2
- down_weight: bfloat16 [3072, 768], P('tensor'), may hold values from -0.109375 to 0.109375
- down_bias: bfloat16 [768], replicated, may hold values from -2 to 2
- ln2_gain: bfloat16 [768], replicated, may hold values from 0.25 to 1.75
- ln2_bias: bfloat16 [768], replicated, may hold values from -2 to 2
Outputs:
- layer_output: bfloat16 [8192, 768], P(('dp', 'tensor'))
- char_table_grad: float32 [262, 16], replicated
- conv_weight_grad: float32 [112, 2048], P(None, ('dp', 'tensor'))
- conv_bias_grad: float32 [2048], P(('dp', 'tensor'))
- highway_weight_grad: float32 [2, 2048, 2, 2048], P(None, None, None, ('dp', 'tensor'))
- highway_bias_grad: float32 [2, 2, 2048], P(None, None, ('dp', 'tensor'))
- proj_weight_grad: float32 [2048, 768], P(('dp', 'tensor'))
- proj_bias_grad: float32 [768], replicated
- qkv_weight_grad: float32 [768, 3, 768], P('dp', None, 'tensor')
- qv_bias_grad: float32 [2, 768], P(None, 'tensor')
- out_weight_grad: float32 [768, 768], P('tensor', 'dp')
- out_bias_grad: float32 [768], replicated
- ln1_gain_grad: float32 [768], replicated
- ln1_bias_grad: float32 [768], replicated
- up_weight_grad: float32 [768, 3072], P('dp', 'tensor')
- up_bias_grad: float32 [3072], P('tensor')
- down_weight_grad: float32 [3072, 768], P('tensor', 'dp')
- down_bias_grad: float32 [768], replicated
- ln2_gain_grad: float32 [768], replicated
- ln2_bias_grad: float32 [768], replicated
The draws below stay inside these ranges and needn't reach their ends.
Inputs may be any that keep to these rules, and one draw needn't show every extreme that they name: `mask_pos`: positions within a sequence; a position may occur twice, its gradients then add. `char_ids`: every character slot of every word holds an id.
All inputs are finite; a program needn't handle non-finite values.
Results may differ from the reference program's by a relative error of at most 0.02.
Values may be sent and summed in bfloat16 or wider, within the bound.
A program may use at most 320 MiB of HBM per device.

```python
import math
import jax
import jax.numpy as jnp
from jax import lax

HEADS = 12
HEAD_DIM = 64
FF = 3072
FILTERS = 2048
CHAR_DIM = 16
CHAR_IDS = 262
CHARS = 50
MAX_WIDTH = 7
HIGHWAYS = 2
LEN = 512
D = 768
MASKED = 76
SEQS = 16
WORDS = 8192


def plant(entries, stream_key, smallest, top_value):
    index_at = [jax.random.randint(jax.random.fold_in(stream_key, axis), (), 0, length) for axis, length in enumerate(entries.shape)]
    longest = entries.shape.index(max(entries.shape))
    neighbour = index_at[:longest] + [(index_at[longest] + 1) % entries.shape[longest]] + index_at[longest + 1:]
    return entries.at[tuple(index_at)].set(smallest).at[tuple(neighbour)].set(top_value)


def steps_of(rng, dims, split, smallest, largest):
    factor_of = 1.0
    for position, blocks in split:
        steps = jax.random.uniform(jax.random.fold_in(jax.random.fold_in(rng, 6), position), (blocks,), jnp.float32, smallest / len(split), largest / len(split))
        factor_of = factor_of * jnp.repeat(jnp.exp(steps), dims[position] // blocks).reshape((-1,) + (1,) * (len(dims) - 1 - position))
    return factor_of


def scatter_about(key, dims, scale, reach, shards=(), kind=jnp.bfloat16):
    factor_of = steps_of(key, dims, shards, -0.22, 0.18) if shards else 1.0
    drawn = jax.random.normal(key, dims, jnp.float32) * scale * factor_of
    return jnp.minimum(jnp.maximum(drawn, -reach), reach).astype(kind)


def setup_inputs(seed: int = 0) -> dict:
    key_list = jax.random.split(jax.random.key(seed), 23)
    char_ids = plant(jax.random.randint(key_list[0], (WORDS, CHARS), 0, CHAR_IDS), jax.random.fold_in(key_list[0], 1), 0, CHAR_IDS - 1).astype(jnp.int32)
    mask_pos = plant(jax.random.randint(key_list[1], (SEQS, MASKED), 0, LEN), jax.random.fold_in(key_list[1], 1), 0, LEN - 1).astype(jnp.int32)
    out_grad = scatter_about(key_list[2], (SEQS, MASKED, D), 1.0, 6.0, ((0, 16),), jnp.float32)
    char_table = scatter_about(key_list[3], (CHAR_IDS, CHAR_DIM), 1.0, 6.0)
    conv_weight = scatter_about(key_list[4], (MAX_WIDTH * CHAR_DIM, FILTERS), CHAR_DIM ** -0.5, 1.5, ((1, 32),))
    conv_bias = jnp.clip(-8.0 + 6.0 * jax.random.uniform(key_list[5], (FILTERS,), jnp.float32) ** steps_of(key_list[5], (FILTERS,), ((0, 32),), -0.2, 0.2), -8.0, -2.0).astype(jnp.bfloat16)
    highway_weight = scatter_about(key_list[6], (HIGHWAYS, FILTERS, 2, FILTERS), FILTERS ** -0.5, 0.125, ((3, 32),))
    highway_bias = scatter_about(key_list[7], (HIGHWAYS, 2, FILTERS), 0.5, 3.0, ((2, 32),))
    proj_weight = scatter_about(key_list[8], (FILTERS, D), (4 * FILTERS) ** -0.5, 0.0625, ((0, 32),))
    proj_bias = scatter_about(key_list[9], (D,), 0.3, 2.0)
    qkv_weight = scatter_about(key_list[10], (D, 3, D), D ** -0.5, 0.21875, ((2, 2),))
    qv_bias = scatter_about(key_list[11], (2, D), 0.3, 2.0, ((1, 2),))
    out_weight = scatter_about(key_list[12], (D, D), (max(3 * D // LEN, 1)) ** -0.5, 3.0, ((0, 2),))
    out_bias = scatter_about(key_list[13], (D,), 0.3, 2.0)
    ln1_gain = jnp.clip(1.0 + 0.15 * jax.random.normal(key_list[14], (D,), jnp.float32), 0.25, 1.75).astype(jnp.bfloat16)
    ln1_bias = scatter_about(key_list[15], (D,), 0.3, 2.0)
    up_weight = scatter_about(key_list[16], (D, FF), D ** -0.5, 0.21875, ((1, 2),))
    up_bias = scatter_about(key_list[17], (FF,), 0.3, 2.0, ((0, 2),))
    down_weight = scatter_about(key_list[18], (FF, D), FF ** -0.5, 0.109375, ((0, 2),))
    down_bias = scatter_about(key_list[19], (D,), 0.3, 2.0)
    ln2_gain = jnp.clip(1.0 + 0.15 * jax.random.normal(key_list[20], (D,), jnp.float32), 0.25, 1.75).astype(jnp.bfloat16)
    ln2_bias = scatter_about(key_list[21], (D,), 0.3, 2.0)
    return dict(char_ids=char_ids, mask_pos=mask_pos, out_grad=out_grad, char_table=char_table, conv_weight=conv_weight, conv_bias=conv_bias, highway_weight=highway_weight, highway_bias=highway_bias, proj_weight=proj_weight, proj_bias=proj_bias, qkv_weight=qkv_weight, qv_bias=qv_bias, out_weight=out_weight, out_bias=out_bias, ln1_gain=ln1_gain, ln1_bias=ln1_bias, up_weight=up_weight, up_bias=up_bias, down_weight=down_weight, down_bias=down_bias, ln2_gain=ln2_gain, ln2_bias=ln2_bias)


@jax.custom_vjp
def low(v):
    return lax.optimization_barrier(v.astype(jnp.bfloat16)).astype(jnp.float32)

@jax.custom_vjp
def low_back(v):
    return v

def low_keep(v):
    return (low(v), None)

def low_pass(kept, grad):
    return (grad,)

def back_keep(v):
    return (v, None)

def back_low(kept, grad):
    return (low(grad),)
low.defvjp(low_keep, low_pass)
low_back.defvjp(back_keep, back_low)
channel_shares = (1, 2, 4, 8, 16, 32)
norm_eps = 1e-05
big_negative = -1e+30
highest = lax.Precision.HIGHEST

def exact_gelu(inputs):
    return jax.nn.gelu(inputs, approximate=False)

def channel_masks():
    channel = jnp.arange(FILTERS, dtype=jnp.int32)
    bounds = jnp.array([portion * (FILTERS // 64) for portion in channel_shares], dtype=jnp.int32)
    filter_width = 1 + lax.optimization_barrier(jnp.sum((channel[:, None] >= bounds[None, :]).astype(jnp.int32), axis=1))
    row_shift = jnp.arange(MAX_WIDTH * CHAR_DIM, dtype=jnp.int32) // CHAR_DIM
    weight_mask = (row_shift[:, None] < filter_width[None, :]).astype(jnp.float32)
    positions = jnp.arange(CHARS, dtype=jnp.int32)
    place_mask = positions[:, None] + filter_width[None, :] <= CHARS
    return (weight_mask, place_mask)

def char_windows(vectors):
    padded = jnp.pad(vectors, ((0, 0), (0, MAX_WIDTH - 1), (0, 0)))
    return jnp.concatenate([padded[:, offset:offset + CHARS, :] for offset in range(MAX_WIDTH)], axis=2)

def layer_norm(summed, gain_vec, bias_vec):
    row_mean = lax.optimization_barrier(jnp.mean(summed, axis=-1, keepdims=True))
    centred = summed - row_mean
    variance = lax.optimization_barrier(jnp.mean(centred * centred, axis=-1, keepdims=True))
    return centred * lax.rsqrt(variance + norm_eps) * gain_vec + bias_vec

def embed_words(params, word_chars):
    char_table, conv_weight, conv_bias, highway_weight, highway_bias, proj_weight, proj_bias = params[:7]
    weight_mask, place_mask = channel_masks()
    char_vectors = low_back(char_table[word_chars])
    windows = char_windows(char_vectors)
    conv_out = low_back(jnp.einsum('wcr,rf->wcf', windows, conv_weight * weight_mask, precision=highest) + conv_bias)
    masked = jnp.where(place_mask[None], conv_out, big_negative)
    row_max = lax.optimization_barrier(jnp.max(masked, axis=1, keepdims=True))
    pooled = (row_max + jnp.log(lax.optimization_barrier(jnp.sum(jnp.exp(masked - row_max), axis=1, keepdims=True))))[:, 0, :]
    highway_state = exact_gelu(pooled)
    for layer_index in range(HIGHWAYS):
        layer_matrix = highway_weight[layer_index].reshape(FILTERS, 2 * FILTERS)
        layer_bias = highway_bias[layer_index].reshape(2 * FILTERS)
        pre_act = low_back(jnp.dot(low(highway_state), layer_matrix, precision=highest) + layer_bias)
        gate_open = jax.nn.sigmoid(pre_act[:, FILTERS:])
        highway_state = gate_open * highway_state + (1.0 - gate_open) * exact_gelu(pre_act[:, :FILTERS])
    return low_back(jnp.dot(low(highway_state), proj_weight, precision=highest) + proj_bias)

def encode_sequence(params, embedded):
    qkv_weight, qv_bias, out_weight, out_bias, ln1_gain, ln1_bias, up_weight, up_bias, down_weight, down_bias, ln2_gain, ln2_bias = params[7:]
    qkv_bias = jnp.stack([qv_bias[0], jnp.zeros_like(qv_bias[0]), qv_bias[1]])
    projected = jnp.einsum('rd,dkw->rkw', low(embedded), qkv_weight, precision=highest) + qkv_bias[None]
    projected = low(low_back(projected))
    queries = projected[:, 0].reshape(LEN, HEADS, HEAD_DIM)
    keys_all = projected[:, 1].reshape(LEN, HEADS, HEAD_DIM)
    values_all = projected[:, 2].reshape(LEN, HEADS, HEAD_DIM)
    score_scale = 1.0 / math.sqrt(HEAD_DIM)
    scores = low_back(jnp.einsum('qhd,khd->hqk', queries, keys_all, precision=highest) * score_scale)
    row_max = lax.optimization_barrier(jnp.max(scores, axis=-1, keepdims=True))
    exp_terms = jnp.exp(scores - row_max)
    attn_probs = exp_terms / lax.optimization_barrier(jnp.sum(exp_terms, axis=-1, keepdims=True))
    mixed_heads = jnp.einsum('hqk,khd->qhd', low(attn_probs), values_all, precision=highest).reshape(LEN, D)
    mixed_heads = low(low_back(mixed_heads))
    attended = low_back(jnp.dot(mixed_heads, out_weight, precision=highest) + out_bias)
    normed = layer_norm(embedded + attended, ln1_gain, ln1_bias)
    hidden_pre = low_back(jnp.dot(low(normed), up_weight, precision=highest) + up_bias)
    hidden_act = low(exact_gelu(hidden_pre))
    ffn_out = low_back(jnp.dot(hidden_act, down_weight, precision=highest) + down_bias)
    return layer_norm(normed + ffn_out, ln2_gain, ln2_bias)

def reference(char_ids, mask_pos, out_grad, char_table, conv_weight, conv_bias, highway_weight, highway_bias, proj_weight, proj_bias, qkv_weight, qv_bias, out_weight, out_bias, ln1_gain, ln1_bias, up_weight, up_bias, down_weight, down_bias, ln2_gain, ln2_bias):
    params = tuple((weight.astype(jnp.float32) for weight in (char_table, conv_weight, conv_bias, highway_weight, highway_bias, proj_weight, proj_bias, qkv_weight, qv_bias, out_weight, out_bias, ln1_gain, ln1_bias, up_weight, up_bias, down_weight, down_bias, ln2_gain, ln2_bias)))
    block_rows = math.gcd(LEN, 256)

    def forward(params):
        word_blocks = char_ids.reshape(-1, block_rows, CHARS)
        embedded = lax.map(jax.checkpoint(lambda word_block: embed_words(params, word_block)), word_blocks)
        embedded = embedded.reshape(SEQS, LEN, D)
        return lax.map(jax.checkpoint(lambda sequence: encode_sequence(params, sequence)), embedded)
    layer_out, pullback = jax.vjp(forward, params)
    seq_rows = jnp.arange(SEQS, dtype=jnp.int32)[:, None] * LEN + mask_pos
    cotangent = jnp.zeros((SEQS * LEN, D), jnp.float32).at[seq_rows.reshape(-1)].add(out_grad.reshape(-1, D).astype(jnp.float32))
    all_grads = pullback(cotangent.reshape(SEQS, LEN, D))[0]
    return (layer_out.reshape(SEQS * LEN, D).astype(jnp.bfloat16), all_grads[0], all_grads[1], all_grads[2], all_grads[3], all_grads[4], all_grads[5], all_grads[6], all_grads[7], all_grads[8], all_grads[9], all_grads[10], all_grads[11], all_grads[12], all_grads[13], all_grads[14], all_grads[15], all_grads[16], all_grads[17], all_grads[18])
```

```python
import functools
import math

import jax
import jax.numpy as jnp
from jax import lax
from jax.experimental import pallas as pl
from jax.experimental.pallas import tpu as pltpu
from jax.sharding import PartitionSpec as P

HEAD_DIM = 64
FILTERS = 2048
CHAR_DIM = 16
CHARS = 50
MAX_WIDTH = 7
LEN = 512
D = 768

channel_shares = (1, 2, 4, 8, 16, 32)
norm_eps = 1e-05
big_negative = -1e30
f32 = jnp.float32
bf16 = jnp.bfloat16
PAIR = "tensor"
GROUP = "dp"
TAPS = 128
VROWS = (CHARS + 7) * CHAR_DIM
FBLOCK = 256


def gelu(x):
    return jax.nn.gelu(x, approximate=False)


def gelu_slope(x):
    return 0.5 * (1.0 + lax.erf(x * (1.0 / math.sqrt(2.0)))) + x * jnp.exp(-0.5 * x * x) * (
        1.0 / math.sqrt(2.0 * math.pi)
    )


def width_of(channel):
    return 1 + sum(channel >= part * (FILTERS // 64) for part in channel_shares)


def dot(a, b, ca, cb):
    return lax.dot_general(a, b, (((ca,), (cb,)), ((), ())), preferred_element_type=f32)


def block_limits(per, start, stop):
    widths = [
        width_of((row // per) * 2 * per + side * per + row % per)
        for row in range(start, stop)
        for side in range(2)
    ]
    return CHARS + 1 - max(widths), CHARS + 1 - min(widths)


MESH = pl.DeviceIdType.MESH
ANYWHERE = pl.BlockSpec(memory_space=pl.ANY)


def pair_swap(x):
    return lax.ppermute(x, PAIR, [(0, 1), (1, 0)])


class Place:
    def __init__(self, lines):
        self.lines = lines
        index = lax.axis_index(GROUP)
        self.side = lax.axis_index(PAIR)
        self.line, self.row, self.core = index // 4, (index // 2) % 2, index % 2
        self.sibling = self.at(self.line, self.row, 1 - self.core)
        self.across = self.at(self.line, 1 - self.row, self.core)
        self.partner = (index, 1 - self.side)

    def at(self, line, row, core):
        return ((line * 2 + row) * 2 + core, self.side)

    def on_line(self, line):
        return self.at(line, self.row, self.core)


def send(source, target, sems, device):
    copy = pltpu.make_async_remote_copy(
        src_ref=source, dst_ref=target, send_sem=sems[0], recv_sem=sems[1],
        device_id=device, device_id_type=MESH,
    )
    copy.start()
    return copy


def meet(devices):
    barrier = pltpu.get_barrier_semaphore()
    for device in devices:
        pl.semaphore_signal(barrier, inc=1, device_id=device, device_id_type=MESH)
    pl.semaphore_wait(barrier, len(devices))


class Gather:
    def __init__(self, place, blocks, wholes, sems):
        self.place, self.blocks, self.wholes = place, blocks, wholes
        self.line_s, self.line_r, self.row_s, self.row_r, self.core_s, self.core_r, self.own = sems

    def piece(self, k, line, row, core):
        return self.wholes[k].at[line, row, core]

    def to_line(self, k, source, line, step):
        p = self.place
        return pltpu.make_async_remote_copy(
            src_ref=source, dst_ref=self.piece(k, line, p.row, p.core),
            send_sem=self.line_s.at[k, line, 0 if step > 0 else 1], recv_sem=self.line_r.at[k, line],
            device_id=p.on_line(lax.rem(p.line + step + p.lines, p.lines)), device_id_type=MESH,
        )

    def to_row(self, k, source, line):
        p = self.place
        return pltpu.make_async_remote_copy(
            src_ref=source, dst_ref=self.piece(k, line, p.row, p.core),
            send_sem=self.row_s.at[k, line], recv_sem=self.row_r.at[k, line],
            device_id=p.across, device_id_type=MESH,
        )

    def to_core(self, k, source, line, row):
        p = self.place
        return pltpu.make_async_remote_copy(
            src_ref=source, dst_ref=self.piece(k, line, row, p.core),
            send_sem=self.core_s.at[k, line, row], recv_sem=self.core_r.at[k, line, row],
            device_id=p.sibling, device_id_type=MESH,
        )

    def pass_on(self, k, line, source, left, right):
        p = self.place
        if right:
            @pl.when(p.line < p.lines - 1)
            def _():
                self.to_line(k, source, line, 1).start()
        if left:
            @pl.when(p.line > 0)
            def _():
                self.to_line(k, source, line, -1).start()
        self.to_row(k, source, line).start()
        self.to_core(k, source, line, p.row).start()

    def begin(self, k):
        p = self.place
        pltpu.make_async_copy(self.blocks[k], self.piece(k, p.line, p.row, p.core), self.own.at[k]).start()
        self.pass_on(k, p.line, self.blocks[k], True, True)

    def from_row(self, k, line):
        p = self.place
        got = self.piece(k, line, 1 - p.row, p.core)
        pltpu.make_async_remote_copy(
            src_ref=got, dst_ref=got, send_sem=self.row_s.at[k, line], recv_sem=self.row_r.at[k, line],
            device_id=p.across, device_id_type=MESH,
        ).wait_recv()
        self.to_core(k, got, line, 1 - p.row).start()

    def turn(self, k, r):
        p = self.place
        for step in (1, -1):
            line = p.line - step * r
            inside = (line >= 0) & (line < p.lines)

            @pl.when(inside)
            def _(line=line, step=step):
                got = self.piece(k, line, p.row, p.core)
                self.to_line(k, got, line, step).wait_recv()
                self.pass_on(k, line, got, step < 0, step > 0)
        self.crossed(k, r - 1)

    def crossed(self, k, r):
        p = self.place
        for step in (1, -1) if r else (1,):
            line = p.line - step * r
            inside = (line >= 0) & (line < p.lines)

            @pl.when(inside)
            def _(line=line):
                self.from_row(k, line)

    def finish(self, k):
        p = self.place
        self.crossed(k, p.lines - 1)
        own = self.piece(k, p.line, p.row, p.core)
        pltpu.make_async_copy(self.blocks[k], own, self.own.at[k]).wait()

        def each(line, carry):
            for row in range(2):
                self.to_core(k, self.piece(k, line, row, p.core), line, row).wait_send()
                self.to_core(k, self.piece(k, line, row, 1 - p.core), line, row).wait_recv()
            self.to_row(k, self.piece(k, line, p.row, p.core), line).wait_send()

            @pl.when((p.line < p.lines - 1) & (line <= p.line))
            def _():
                self.to_line(k, self.piece(k, line, p.row, p.core), line, 1).wait_send()

            @pl.when((p.line > 0) & (line >= p.line))
            def _():
                self.to_line(k, self.piece(k, line, p.row, p.core), line, -1).wait_send()
            return carry

        lax.fori_loop(0, p.lines, each, 0)

    @staticmethod
    def sems(count, lines):
        dma = pltpu.SemaphoreType.DMA
        return [
            dma((count, lines, 2)), dma((count, lines)), dma((count, lines)), dma((count, lines)),
            dma((count, lines, 2)), dma((count, lines, 2)), dma((count,)),
        ]


def neighbours(place, partner):
    others = [
        place.on_line(lax.rem(place.line + step, place.lines)) for step in range(1, place.lines)
    ]
    return [place.sibling, place.across, *others] + ([place.partner] if partner else [])


def gather_kernel(lines, count, swap, *refs):
    blocks, refs = refs[:count], refs[count:]
    swap_in, refs = refs[:swap], refs[swap:]
    wholes, refs = refs[:count], refs[count:]
    swap_out, refs = refs[:swap], refs[swap:]
    place = Place(lines)
    gather = Gather(place, blocks, wholes, refs[:7])
    meet(neighbours(place, bool(swap)))
    for k in range(count):
        gather.begin(k)
    if swap:
        copy = send(swap_in[0], swap_out[0], refs[7:9], place.partner)
    for r in range(1, lines):
        for k in range(count):
            gather.turn(k, r)
    for k in range(count):
        gather.finish(k)
    if swap:
        copy.wait()


def gather_blocks(blocks, lines, ident, swap=None):
    count = len(blocks)
    swaps = [] if swap is None else [swap]
    dma = pltpu.SemaphoreType.DMA
    outs = pl.pallas_call(
        functools.partial(gather_kernel, lines, count, len(swaps)),
        out_shape=tuple(
            [jax.ShapeDtypeStruct((lines, 2, 2) + b.shape, b.dtype) for b in blocks]
            + [jax.ShapeDtypeStruct(s.shape, s.dtype) for s in swaps]
        ),
        in_specs=[ANYWHERE] * (count + len(swaps)),
        out_specs=tuple([ANYWHERE] * (count + len(swaps))),
        scratch_shapes=Gather.sems(count, lines) + [dma, dma] * len(swaps),
        compiler_params=pltpu.CompilerParams(collective_id=ident, has_side_effects=True),
    )(*blocks, *swaps)
    return [o.reshape((4 * lines,) + b.shape) for o, b in zip(outs, blocks)] + list(outs[count:])


class Scatter:
    def __init__(self, place, arrays, from_core, from_row, from_line, outs, pieces, bufs, sems):
        self.place, self.arrays, self.outs, self.pieces = place, arrays, outs, pieces
        self.from_core, self.from_row, self.from_line = from_core, from_row, from_line
        self.mine, self.theirs, self.sums, self.crossed, self.leaving, self.arrived = bufs
        self.core_s, self.core_r, self.row_s, self.row_r, self.line_s, self.line_r, self.load = sems

    def span(self, k):
        array, start, size = self.pieces[k]
        return array, pl.ds(start, size), size, self.arrays[array].shape[-1]

    def core_copy(self, k):
        array, rows, size, width = self.span(k)
        p = self.place
        return pltpu.make_async_remote_copy(
            src_ref=self.arrays[array].at[:, :, 1 - p.core, rows],
            dst_ref=self.from_core[array].at[:, :, rows],
            send_sem=self.core_s.at[k], recv_sem=self.core_r.at[k],
            device_id=p.sibling, device_id_type=MESH,
        )

    def row_copy(self, k):
        array, rows, size, width = self.span(k)
        p = self.place
        return pltpu.make_async_remote_copy(
            src_ref=self.sums.at[k % self.sums.shape[0], 1 - p.row, :, pl.ds(0, size), pl.ds(0, width)],
            dst_ref=self.from_row[array].at[:, rows],
            send_sem=self.row_s.at[k], recv_sem=self.row_r.at[k],
            device_id=p.across, device_id_type=MESH,
        )

    def line_copy(self, k, step):
        array, rows, size, width = self.span(k)
        p = self.place
        line = lax.rem(p.line + step, p.lines)
        return pltpu.make_async_remote_copy(
            src_ref=self.leaving.at[k % self.leaving.shape[0], line, pl.ds(0, size), pl.ds(0, width)],
            dst_ref=self.from_line[array].at[step, rows],
            send_sem=self.line_s.at[k, step], recv_sem=self.line_r.at[k, step],
            device_id=p.on_line(line), device_id_type=MESH,
        )

    def begin(self, k):
        self.core_copy(k).start()

    def add_core(self, k):
        array, rows, size, width = self.span(k)
        p = self.place
        slot = k % self.sums.shape[0]
        if k >= self.sums.shape[0]:
            self.row_copy(k - self.sums.shape[0]).wait_send()
        here = (slice(None), slice(None), pl.ds(0, size), pl.ds(0, width))
        mine = pltpu.make_async_copy(
            self.arrays[array].at[:, :, p.core, rows], self.mine.at[here], self.load.at[0]
        )
        mine.start()
        self.core_copy(k).wait_recv()
        theirs = pltpu.make_async_copy(
            self.from_core[array].at[:, :, rows], self.theirs.at[here], self.load.at[1]
        )
        theirs.start()
        mine.wait()
        theirs.wait()

        def each(i, carry):
            line = i // (size // 16)
            part = pl.ds(pl.multiple_of((i % (size // 16)) * 16, 16), 16)
            for row in range(2):
                total = self.mine[line, row, part, :width].astype(f32) + self.theirs[
                    line, row, part, :width
                ].astype(f32)
                self.sums[slot, row, line, part, :width] = total.astype(bf16)
            return carry

        lax.fori_loop(0, p.lines * (size // 16), each, 0)
        self.row_copy(k).start()

    def add_row(self, k):
        array, rows, size, width = self.span(k)
        p = self.place
        slot = k % self.sums.shape[0]
        away = k % self.leaving.shape[0]
        if k >= self.leaving.shape[0]:
            for step in range(1, p.lines):
                self.line_copy(k - self.leaving.shape[0], step).wait_send()
        here = (slice(None), pl.ds(0, size), pl.ds(0, width))
        self.row_copy(k).wait_recv()
        copy = pltpu.make_async_copy(
            self.from_row[array].at[:, rows], self.crossed.at[here], self.load.at[2]
        )
        copy.start()
        copy.wait()

        def each(i, carry):
            line = i // (size // 16)
            part = pl.ds(pl.multiple_of((i % (size // 16)) * 16, 16), 16)
            total = self.sums[slot, p.row, line, part, :width].astype(f32) + self.crossed[
                line, part, :width
            ].astype(f32)
            self.leaving[away, line, part, :width] = total.astype(bf16)
            return carry

        lax.fori_loop(0, p.lines * (size // 16), each, 0)
        for step in range(1, p.lines):
            self.line_copy(k, step).start()
        own = self.leaving.at[away, p.line, pl.ds(0, size), pl.ds(0, width)]
        copy = pltpu.make_async_copy(own, self.from_line[array].at[0, rows], self.load.at[3])
        copy.start()
        copy.wait()

    def add_line(self, k):
        array, rows, size, width = self.span(k)
        start = self.pieces[k][1]
        p = self.place
        for step in range(1, p.lines):
            self.line_copy(k, step).wait_recv()
        here = (slice(None), pl.ds(0, size), pl.ds(0, width))
        copy = pltpu.make_async_copy(
            self.from_line[array].at[:, rows], self.arrived.at[here], self.load.at[4]
        )
        copy.start()
        copy.wait()

        def each(i, carry):
            part = pl.ds(pl.multiple_of(i * 16, 16), 16)
            total = self.arrived[0, part, :width].astype(f32)
            for step in range(1, p.lines):
                total = total + self.arrived[step, part, :width].astype(f32)
            self.outs[array][pl.ds(pl.multiple_of(start + i * 16, 16), 16), :] = total
            return carry

        lax.fori_loop(0, size // 16, each, 0)

    def steps(self):
        count = len(self.pieces)
        work = []
        for k in range(count + 4):
            if k < count:
                work.append(functools.partial(self.add_core, k))
            if 0 <= k - 2 < count:
                work.append(functools.partial(self.add_row, k - 2))
            if 0 <= k - 4 < count:
                work.append(functools.partial(self.add_line, k - 4))
        return work

    def finish(self):
        count = len(self.pieces)
        for k in range(count):
            self.core_copy(k).wait_send()
            if k >= count - self.sums.shape[0]:
                self.row_copy(k).wait_send()
            if k >= count - self.leaving.shape[0]:
                for step in range(1, self.place.lines):
                    self.line_copy(k, step).wait_send()

    @staticmethod
    def shapes(arrays, pieces, lines):
        land = []
        for lead in ((lines, 2), (lines,), (lines,)):
            land += [jax.ShapeDtypeStruct(lead + a.shape[3:], bf16) for a in arrays]
        outs = [jax.ShapeDtypeStruct(a.shape[3:], f32) for a in arrays]
        rows = max(size for _, _, size in pieces)
        width = max(a.shape[-1] for a in arrays)
        dma = pltpu.SemaphoreType.DMA
        count = len(pieces)
        bufs = [
            pltpu.VMEM((lines, 2, rows, width), bf16), pltpu.VMEM((lines, 2, rows, width), bf16),
            pltpu.VMEM((3, 2, lines, rows, width), bf16), pltpu.VMEM((lines, rows, width), bf16),
            pltpu.VMEM((2, lines, rows, width), bf16), pltpu.VMEM((lines, rows, width), bf16),
        ]
        sems = [dma((count,))] * 4 + [dma((count, lines))] * 2 + [dma((5,))]
        return land, outs, bufs, sems


def scatter_kernel(lines, count, pieces, swap, *refs):
    arrays, refs = refs[:count], refs[count:]
    swap_in, refs = refs[:swap], refs[swap:]
    land, refs = refs[: 3 * count], refs[3 * count :]
    outs, refs = refs[:count], refs[count:]
    swap_out, refs = refs[:swap], refs[swap:]
    place = Place(lines)
    scatter = Scatter(
        place, arrays, land[:count], land[count : 2 * count], land[2 * count :], outs, pieces,
        refs[:6], refs[6:13],
    )
    meet(neighbours(place, bool(swap)))
    if swap:
        copy = send(swap_in[0], swap_out[0], refs[13:15], place.partner)
    for k in range(len(pieces)):
        scatter.begin(k)
    for step in scatter.steps():
        step()
    scatter.finish()
    if swap:
        copy.wait()


def cut(arrays, most):
    pieces = []
    for i, a in enumerate(arrays):
        rows = a.shape[3]
        size = max(s for s in range(16, most + 1, 16) if rows % s == 0)
        pieces += [(i, start, size) for start in range(0, rows, size)]
    return pieces


def scatter_blocks(arrays, lines, ident, most=48, swap=None):
    whole = []
    for a in arrays:
        rows = -(-a.shape[1] // 16) * 16
        a = jnp.pad(a.astype(bf16), ((0, 0), (0, rows - a.shape[1]), (0, 0)))
        whole.append(a.reshape((lines, 2, 2) + a.shape[1:]))
    pieces = cut(whole, most)
    land, outs, bufs, sems = Scatter.shapes(whole, pieces, lines)
    swaps = [] if swap is None else [swap]
    dma = pltpu.SemaphoreType.DMA
    count = len(arrays)
    result = pl.pallas_call(
        functools.partial(scatter_kernel, lines, count, pieces, len(swaps)),
        out_shape=tuple(land + outs + [jax.ShapeDtypeStruct(s.shape, s.dtype) for s in swaps]),
        in_specs=[ANYWHERE] * (count + len(swaps)),
        out_specs=tuple(
            [ANYWHERE] * len(land)
            + [pl.BlockSpec(memory_space=pltpu.VMEM)] * count
            + [ANYWHERE] * len(swaps)
        ),
        scratch_shapes=bufs + sems + [dma, dma] * len(swaps),
        compiler_params=pltpu.CompilerParams(
            collective_id=ident, has_side_effects=True, vmem_limit_bytes=48 << 20
        ),
    )(*whole, *swaps)
    own = [r[: a.shape[1]] for r, a in zip(result[3 * count : 4 * count], arrays)]
    return own + list(result[4 * count :])


def total_kernel(lines, x_ref, o_ref, inbox, send_sems, recv_sems):
    place = Place(lines)
    partners = [place.sibling, place.across]
    span = 1
    while span < lines:
        low = lax.rem(place.line // span, 2)
        partners.append(place.on_line(place.line + span - 2 * span * low))
        span *= 2
    partners.append(place.partner)
    meet(partners)
    o_ref[...] = x_ref[...]
    for i, device in enumerate(partners):
        copy = send(o_ref, inbox.at[i], (send_sems.at[i], recv_sems.at[i]), device)
        copy.wait()
        o_ref[...] = o_ref[...] + inbox[i]


def total_all(x, lines, ident):
    count = 3 + (lines - 1).bit_length()
    dma = pltpu.SemaphoreType.DMA
    vmem = pl.BlockSpec(memory_space=pltpu.VMEM)
    return pl.pallas_call(
        functools.partial(total_kernel, lines),
        out_shape=jax.ShapeDtypeStruct(x.shape, x.dtype),
        in_specs=[vmem],
        out_specs=vmem,
        scratch_shapes=[pltpu.VMEM((count,) + x.shape, x.dtype), dma((count,)), dma((count,))],
        compiler_params=pltpu.CompilerParams(collective_id=ident, has_side_effects=True),
    )(x)


def onehot_chars(ids_row, count):
    return jnp.where(
        lax.broadcasted_iota(jnp.int32, (count, ids_row.shape[1]), 0) == ids_row, 1.0, 0.0
    ).astype(bf16)


def conv_forward_kernel(limits, ids_ref, table_ref, weight_ref, lim_ref, pooled_ref, chars_ref, conv_ref):
    words = ids_ref.shape[1]
    count = table_ref.shape[1]

    def embed(c, carry):
        hot = onehot_chars(ids_ref[pl.ds(c, 1), :], count)
        vec = dot(table_ref[...], hot, 1, 0)
        chars_ref[pl.ds(pl.multiple_of(c * CHAR_DIM, CHAR_DIM), CHAR_DIM), :] = vec.astype(bf16)
        return carry

    lax.fori_loop(0, CHARS, embed, 0)
    chars_ref[CHARS * CHAR_DIM :, :] = jnp.zeros((VROWS - CHARS * CHAR_DIM, words), bf16)

    for block, (full, some) in enumerate(limits):
        rows = pl.ds(block * FBLOCK, FBLOCK)
        for half in range(words // FBLOCK):
            lanes = pl.ds(half * FBLOCK, FBLOCK)

            def convolve(p, carry):
                taps = chars_ref[pl.ds(pl.multiple_of(p * CHAR_DIM, CHAR_DIM), TAPS), lanes]
                conv_ref[p] = dot(weight_ref[rows, :], taps, 1, 0)
                return carry

            lax.fori_loop(0, some, convolve, 0)

            def pool(g, carry):
                here = pl.ds(pl.multiple_of(g * 8, 8), 8)
                there = pl.ds(pl.multiple_of(block * FBLOCK + g * 8, 8), 8)
                lim = lim_ref[there, :] if some > full else None

                def entry(p):
                    value = conv_ref[p, here, :]
                    return value if p < full else jnp.where(lim[:, :1] >= p, value, big_negative)

                top = entry(0)
                for p in range(1, some):
                    top = jnp.maximum(top, entry(p))
                total = jnp.exp(entry(0) - top)
                for p in range(1, some):
                    total = total + jnp.exp(entry(p) - top)
                pooled_ref[there, lanes] = top + jnp.log(total)
                return carry

            lax.fori_loop(0, FBLOCK // 8, pool, 0)


def conv_forward(ids, table, weight, lim, per):
    rows = weight.shape[0]
    words = ids.shape[1]
    limits = tuple(block_limits(per, s, s + FBLOCK) for s in range(0, rows, FBLOCK))
    return pl.pallas_call(
        functools.partial(conv_forward_kernel, limits),
        out_shape=(
            jax.ShapeDtypeStruct((rows, words), f32),
            jax.ShapeDtypeStruct((VROWS, words), bf16),
        ),
        scratch_shapes=[pltpu.VMEM((CHARS, FBLOCK, FBLOCK), f32)],
        compiler_params=pltpu.CompilerParams(vmem_limit_bytes=48 << 20),
        cost_estimate=pl.CostEstimate(flops=14 * 10**9, bytes_accessed=8 << 20, transcendentals=24 * 10**6),
    )(ids, table, weight, lim)


def conv_backward_kernel(
    limits, ids_ref, chars_ref, weight_ref, weight_t_ref, lim_ref, pooled_ref, grad_ref,
    weight_grad_ref, table_grad_ref, dconv_ref, dchars_ref,
):
    words = ids_ref.shape[1]
    count = table_grad_ref.shape[1]
    dchars_ref[...] = jnp.zeros_like(dchars_ref)
    weight_grad_ref[...] = jnp.zeros_like(weight_grad_ref)
    table_grad_ref[...] = jnp.zeros_like(table_grad_ref)
    always = min(full for full, some in limits)
    ever = max(some for full, some in limits)

    def place(p, blocks):
        if isinstance(p, int):
            window = pl.ds(p * CHAR_DIM, TAPS)
        else:
            window = pl.ds(pl.multiple_of(p * CHAR_DIM, CHAR_DIM), TAPS)
        for block in blocks:
            full, some = limits[block]
            rows = pl.ds(block * FBLOCK, FBLOCK)
            taps = chars_ref[window, :]
            weights = jnp.exp(dot(weight_ref[rows, :], taps, 1, 0) - pooled_ref[rows, :])
            value = weights * grad_ref[rows, :]
            if isinstance(p, int) and p >= full:
                value = jnp.where(lim_ref[rows, :][:, :1] >= p, value, 0.0)
            value = value.astype(bf16)
            dconv_ref[rows, :] = value
            weight_grad_ref[rows, :] += dot(value, taps, 1, 1)
        count_rows = len(blocks) * FBLOCK
        dchars_ref[window, :] += dot(weight_t_ref[:, :count_rows], dconv_ref[:count_rows, :], 1, 0)

    everyone = range(len(limits))

    def step(p, carry):
        place(p, everyone)
        return carry

    lax.fori_loop(0, always, step, 0)
    for p in range(always, ever):
        blocks = [block for block, (full, some) in enumerate(limits) if p < some]
        place(p, range(max(blocks) + 1))

    def spread(c, carry):
        rows = pl.ds(pl.multiple_of(c * CHAR_DIM, CHAR_DIM), CHAR_DIM)
        hot = onehot_chars(ids_ref[pl.ds(c, 1), :], count)
        table_grad_ref[...] += dot(dchars_ref[rows, :].astype(bf16), hot, 1, 1)
        return carry

    lax.fori_loop(0, CHARS, spread, 0)


def conv_backward(ids, chars, weight, lim, pooled, grad, per, count):
    rows = weight.shape[0]
    words = ids.shape[1]
    limits = tuple(block_limits(per, s, s + FBLOCK) for s in range(0, rows, FBLOCK))
    return pl.pallas_call(
        functools.partial(conv_backward_kernel, limits),
        out_shape=(
            jax.ShapeDtypeStruct((rows, TAPS), f32),
            jax.ShapeDtypeStruct((CHAR_DIM, count), f32),
        ),
        scratch_shapes=[pltpu.VMEM((rows, words), bf16), pltpu.VMEM((VROWS, words), f32)],
        compiler_params=pltpu.CompilerParams(vmem_limit_bytes=48 << 20),
        cost_estimate=pl.CostEstimate(flops=42 * 10**9, bytes_accessed=8 << 20, transcendentals=24 * 10**6),
    )(ids, chars, weight, weight.T, lim, pooled, grad)


def norm_forward(summed):
    centred = summed - jnp.mean(summed, axis=-1, keepdims=True)
    inv_std = lax.rsqrt(jnp.mean(centred * centred, axis=-1, keepdims=True) + norm_eps)
    return centred * inv_std, inv_std


def norm_backward(grad_out, normalized, inv_std, gain):
    grad_norm = grad_out * gain
    return inv_std * (
        grad_norm
        - jnp.mean(grad_norm, axis=-1, keepdims=True)
        - normalized * jnp.mean(grad_norm * normalized, axis=-1, keepdims=True)
    )


def split_two(x):
    high = x.astype(bf16)
    return high, (x - high.astype(f32)).astype(bf16)


def per_device(
    char_ids, mask_pos, out_grad, char_table, conv_weight, conv_bias, highway_weight, highway_bias,
    proj_weight, proj_bias, qkv_weight, qv_bias, out_weight, out_bias, ln1_gain, ln1_bias, up_weight,
    up_bias, down_weight, down_bias, ln2_gain, ln2_bias,
):
    side = lax.axis_index(PAIR)
    per = conv_weight.shape[1]
    ndp = FILTERS // (2 * per)
    rows_here = char_ids.shape[0]
    words = 2 * rows_here
    own = ndp * per
    layers = highway_weight.shape[0]
    ids_count = char_table.shape[0]
    padded_ids = -(-ids_count // 128) * 128

    taps_used = conv_weight.shape[0]
    packed = jnp.concatenate(
        [
            conv_weight.T.astype(f32),
            conv_bias[:, None].astype(f32),
            highway_bias.reshape(2 * layers, per).T.astype(f32),
            jnp.zeros((per, TAPS - taps_used - 1 - 2 * layers), f32),
        ],
        axis=1,
    )
    highway_t = highway_weight.transpose(0, 2, 3, 1)
    lines = ndp // 4
    blocks = [highway_t[i].reshape(2 * per, FILTERS) for i in range(layers)]
    highway_all = [None] * layers
    packed_all, highway_all[0] = gather_blocks([packed, blocks[0]], lines, 1)
    packed_all = packed_all.reshape(own, TAPS)
    highway_all[0] = highway_all[0].reshape(2 * own, FILTERS)

    filter_index = jnp.arange(own, dtype=jnp.int32)
    filter_index = (filter_index // per) * (2 * per) + side * per + filter_index % per
    filter_width = width_of(filter_index).astype(jnp.int32)
    lim = jnp.broadcast_to((CHARS - filter_width)[:, None], (own, 128))
    tap_shift = jnp.arange(TAPS, dtype=jnp.int32) // CHAR_DIM
    conv_all = jnp.where(
        (tap_shift[None, :] < filter_width[:, None]) & (jnp.arange(TAPS) < taps_used)[None, :],
        packed_all,
        0.0,
    ).astype(bf16)
    conv_bias_all = packed_all[:, taps_used][:, None]

    def layer_bias(i):
        both = packed_all[:, taps_used + 1 + 2 * i : taps_used + 3 + 2 * i]
        return both.reshape(ndp, per, 2).transpose(0, 2, 1)[..., None]

    def both_sides(mine, theirs):
        mine = mine.reshape(ndp, 1, per, words)
        theirs = theirs.reshape(ndp, 1, per, words)
        first = jnp.where(side == 0, mine, theirs)
        second = jnp.where(side == 0, theirs, mine)
        return jnp.concatenate([first, second], axis=1).reshape(FILTERS, words)

    ids = lax.all_gather(char_ids.T, PAIR, axis=1, tiled=True)
    table_t = jnp.pad(char_table.T, ((0, 0), (0, padded_ids - ids_count)))
    pooled_raw, chars = conv_forward(ids, table_t, conv_all, lim, per)
    pooled = pooled_raw + conv_bias_all
    state = gelu(pooled)
    kept = []
    for i in range(layers):
        state_low = state.astype(bf16)
        if i == 0:
            *highways, proj_all, other_low = gather_blocks(
                blocks[1:] + [proj_weight], lines, 2, state_low
            )
            highway_all[1:] = [h.reshape(2 * own, FILTERS) for h in highways]
            proj_all = proj_all.reshape(own, D)
        else:
            other_low = pair_swap(state_low)
        state_full = both_sides(state_low, other_low)
        pre = dot(highway_all[i], state_full, 1, 0).reshape(ndp, 2, per, words) + layer_bias(i)
        nonlin = pre[:, 0].reshape(own, words)
        gate = jax.nn.sigmoid(pre[:, 1].reshape(own, words))
        kept.append((state, state_full, nonlin, gate))
        state = gate * state + (1.0 - gate) * gelu(nonlin)
    state_low = state.astype(bf16)
    emb_part = dot(state_low, proj_all, 0, 0)
    embedded = emb_part + pair_swap(emb_part.astype(bf16)).astype(f32) + proj_bias.astype(f32)

    emb_low = embedded.astype(bf16)
    seqs = words // LEN
    width = qkv_weight.shape[2]
    heads = width // HEAD_DIM
    qkv_t = qkv_weight.transpose(1, 0, 2)
    qkv_bias = jnp.stack([qv_bias[0], jnp.zeros_like(qv_bias[0]), qv_bias[1]]).astype(f32)
    projected = [
        (dot(emb_low, qkv_t[part], 1, 0) + qkv_bias[part][None]).astype(bf16) for part in range(3)
    ]

    def by_head(x):
        return x.reshape(-1, heads, HEAD_DIM).transpose(1, 0, 2)

    queries, keys, values = (by_head(part) for part in projected)
    scale = 1.0 / math.sqrt(HEAD_DIM)

    def probs_of(q):
        scores = jnp.einsum("hqd,hkd->hqk", q, keys, preferred_element_type=f32) * scale
        terms = jnp.exp(scores - jnp.max(scores, axis=-1, keepdims=True))
        return terms / jnp.sum(terms, axis=-1, keepdims=True)

    mixed = (
        jnp.einsum("hqk,hkd->qhd", probs_of(queries).astype(bf16), values, preferred_element_type=f32)
        .reshape(words, width)
        .astype(bf16)
    )
    att_part = dot(mixed, out_weight, 1, 0)
    gain_one, gain_two = ln1_gain.astype(f32), ln2_gain.astype(f32)
    summed = embedded + (
        att_part + pair_swap(att_part.astype(bf16)).astype(f32) + out_bias.astype(f32)
    )
    normalized_one, inv_std_one = norm_forward(summed)
    normed = normalized_one * gain_one + ln1_bias.astype(f32)
    normed_low = normed.astype(bf16)
    hidden = gelu(dot(normed_low, up_weight, 1, 0) + up_bias.astype(f32)).astype(bf16)
    ffn_part = dot(hidden, down_weight, 1, 0)

    slots = mask_pos.shape[1]
    padded_slots = -(-slots // 16) * 16
    positions = jnp.pad(mask_pos[0], (0, padded_slots - slots), constant_values=-1)
    pick = (positions[:, None] == jnp.arange(words, dtype=jnp.int32)[None, :]).astype(bf16)
    slot_grad = jnp.pad(out_grad[0], ((0, padded_slots - slots), (0, 0)))
    n1_high, n1_low = split_two(normalized_one)
    n1_s = dot(pick, n1_high, 1, 0) + dot(pick, n1_low, 1, 0)
    r1_s = jnp.sum(jnp.where(pick > 0, inv_std_one.T, 0.0), axis=1, keepdims=True)
    normed_s = n1_s * gain_one + ln1_bias.astype(f32)
    normed_low_s = dot(pick, normed_low, 1, 0).astype(bf16)
    mixed_s = dot(pick, mixed, 1, 0).astype(bf16)
    emb_s = dot(pick, emb_low, 1, 0).astype(bf16)
    queries_s = jnp.einsum("mw,hwd->hmd", pick, queries, preferred_element_type=f32).astype(bf16)
    hidden_pre_s = dot(normed_low_s, up_weight, 1, 0) + up_bias.astype(f32)
    hidden_s = gelu(hidden_pre_s).astype(bf16)
    ffn_s = dot(hidden_s, down_weight, 1, 0)

    theirs = lax.dynamic_slice_in_dim(ffn_part, (1 - side) * rows_here, rows_here, 0)
    got = pair_swap(jnp.concatenate([theirs, ffn_s], axis=0).astype(bf16)).astype(f32)
    start = side * rows_here
    second = (
        lax.dynamic_slice_in_dim(normed, start, rows_here, 0)
        + (lax.dynamic_slice_in_dim(ffn_part, start, rows_here, 0) + got[:rows_here])
        + down_bias.astype(f32)
    )
    normalized_two, _ = norm_forward(second)
    result = normalized_two * gain_two + ln2_bias.astype(f32)
    n2_s, r2_s = norm_forward(normed_s + (ffn_s + got[rows_here:]) + down_bias.astype(f32))

    grad_second = norm_backward(slot_grad, n2_s, r2_s, gain_two)
    ln2_gain_grad = jnp.sum(slot_grad * n2_s, axis=0)
    ln2_bias_grad = jnp.sum(slot_grad, axis=0)
    dffn = grad_second.astype(bf16)
    down_bias_grad = jnp.sum(dffn, axis=0, dtype=f32)
    down_grad_t = dot(dffn, hidden_s, 0, 0)
    dpre = (dot(dffn, down_weight, 1, 1) * gelu_slope(hidden_pre_s)).astype(bf16)
    up_bias_grad = jnp.sum(dpre, axis=0, dtype=f32)
    up_grad = dot(normed_low_s, dpre, 0, 0)
    dn_part = dot(dpre, up_weight, 1, 1)
    grad_normed = grad_second + (dn_part + pair_swap(dn_part.astype(bf16)).astype(f32))
    grad_first = norm_backward(grad_normed, n1_s, r1_s, gain_one)
    ln1_gain_grad = jnp.sum(grad_normed * n1_s, axis=0)
    ln1_bias_grad = jnp.sum(grad_normed, axis=0)
    dattn = grad_first.astype(bf16)
    out_bias_grad = jnp.sum(dattn, axis=0, dtype=f32)
    out_grad_t = dot(dattn, mixed_s, 0, 0)
    dmixed = by_head(dot(dattn, out_weight, 1, 1).astype(bf16))
    probs = probs_of(queries_s)
    dvalues = jnp.einsum("hqk,hqd->khd", probs.astype(bf16), dmixed, preferred_element_type=f32)
    dprobs = jnp.einsum("hqd,hkd->hqk", dmixed, values, preferred_element_type=f32)
    dscores = (probs * (dprobs - jnp.sum(probs * dprobs, axis=-1, keepdims=True))).astype(bf16)
    dqueries = jnp.einsum("hqk,hkd->qhd", dscores, keys, preferred_element_type=f32) * scale
    dkeys = jnp.einsum("hqk,hqd->khd", dscores, queries_s, preferred_element_type=f32) * scale
    dq = dqueries.reshape(padded_slots, width).astype(bf16)
    dk = dkeys.reshape(words, width).astype(bf16)
    dv = dvalues.reshape(words, width).astype(bf16)
    qv_bias_grad = jnp.stack([jnp.sum(dq, axis=0, dtype=f32), jnp.sum(dv, axis=0, dtype=f32)])
    qkvo_grad = [dot(emb_s, dq, 0, 0), dot(emb_low, dk, 0, 0), dot(emb_low, dv, 0, 0), out_grad_t]
    dq_high, dq_low = split_two(dot(dq, qkv_t[0], 1, 1))
    gf_high, gf_low = split_two(grad_first)
    back = dot(pick, jnp.concatenate([dq_high, gf_high], axis=1), 0, 0) + dot(
        pick, jnp.concatenate([dq_low, gf_low], axis=1), 0, 0
    )
    de_part = back[:, :D] + dot(dk, qkv_t[1], 1, 1) + dot(dv, qkv_t[2], 1, 1)
    encoder_grads = [
        g.astype(bf16).reshape(ndp, D // ndp, -1)
        for g in (up_grad, down_grad_t, jnp.concatenate(qkvo_grad, axis=1))
    ]
    up_mine, down_mine, qkvo_mine, de_other = scatter_blocks(
        encoder_grads, lines, 3, swap=de_part.astype(bf16)
    )
    grad_embedded = back[:, D:] + (de_part + de_other.astype(f32))
    demb = grad_embedded.astype(bf16)

    proj_bias_grad = jnp.sum(demb, axis=0, dtype=f32)
    proj_grad = dot(state_low, demb, 1, 0)
    grad_state = dot(proj_all, demb, 1, 1)
    highway_mine = [None] * layers
    highway_bias_grads = [None] * layers
    for i in reversed(range(layers)):
        state_in, state_full, nonlin, gate = kept[i]
        d_nonlin = (grad_state * (1.0 - gate) * gelu_slope(nonlin)).astype(bf16)
        d_gate = (grad_state * (state_in - gelu(nonlin)) * gate * (1.0 - gate)).astype(bf16)
        d_pre = jnp.stack(
            [d_nonlin.reshape(ndp, per, words), d_gate.reshape(ndp, per, words)], axis=1
        ).reshape(2 * own, words)
        highway_grad = dot(d_pre, state_full, 1, 1).astype(bf16).reshape(ndp, 2 * per, FILTERS)
        highway_bias_grads[i] = jnp.sum(d_pre, axis=1, dtype=f32)
        back_part = dot(highway_all[i], d_pre, 0, 0).reshape(ndp, 2, per, words)
        mine = jnp.where(side == 0, back_part[:, 0], back_part[:, 1]).reshape(own, words)
        other = jnp.where(side == 0, back_part[:, 1], back_part[:, 0]).reshape(own, words)
        ready = [highway_grad]
        if i == layers - 1:
            ready.append(proj_grad.astype(bf16).reshape(ndp, per, D))
        highway_mine[i], *rest, theirs = scatter_blocks(ready, lines, 4 + i, swap=other.astype(bf16))
        if rest:
            proj_mine = rest[0]
        grad_state = grad_state * gate + (mine + theirs.astype(f32))
    grad_pooled = grad_state * gelu_slope(pooled)
    conv_bias_grad = jnp.sum(grad_pooled, axis=1)
    conv_grad, table_grad_t = conv_backward(
        ids, chars, conv_all, lim, pooled_raw, grad_pooled, per, padded_ids
    )
    tap_mask = (tap_shift[None, :] < filter_width[:, None])[:, :taps_used]
    conv_grad = jnp.where(tap_mask, conv_grad[:, :taps_used], 0.0)

    bias_grads = [conv_bias_grad[:, None]]
    for i in range(layers):
        both = highway_bias_grads[i].reshape(ndp, 2, per).transpose(0, 2, 1).reshape(own, 2)
        bias_grads.append(both)
    conv_pack = jnp.concatenate(
        [conv_grad, *bias_grads, jnp.zeros((own, TAPS - taps_used - 1 - 2 * layers), f32)], axis=1
    )
    (conv_mine,) = scatter_blocks([conv_pack.reshape(ndp, per, TAPS)], lines, 4 + layers)
    first = side == 0
    shared = [
        jnp.where(first, g, 0.0)
        for g in (
            proj_bias_grad, out_bias_grad, ln1_gain_grad, ln1_bias_grad, down_bias_grad,
            ln2_gain_grad, ln2_bias_grad,
        )
    ]
    own_side = jnp.concatenate([qv_bias_grad.reshape(-1), up_bias_grad])
    flat = jnp.concatenate(
        [
            table_grad_t.reshape(-1),
            *shared,
            jnp.where(first, own_side, 0.0),
            jnp.where(first, 0.0, own_side),
        ]
    )
    rows_flat = -(-flat.shape[0] // 1024) * 8
    flat = jnp.pad(flat, (0, rows_flat * 128 - flat.shape[0])).reshape(rows_flat, 128)
    flat = total_all(flat, lines, 5 + layers).reshape(-1)
    at = table_grad_t.size
    table_grad_t = flat[:at].reshape(table_grad_t.shape)
    (
        proj_bias_grad, out_bias_grad, ln1_gain_grad, ln1_bias_grad, down_bias_grad, ln2_gain_grad,
        ln2_bias_grad,
    ) = (flat[at + i * D : at + (i + 1) * D] for i in range(7))
    at += 7 * D
    size = own_side.shape[0]
    own_side = jnp.where(first, flat[at : at + size], flat[at + size : at + 2 * size])
    qv_bias_grad = own_side[: 2 * width].reshape(2, width)
    up_bias_grad = own_side[2 * width :]
    conv_bias_mine = conv_mine[:, taps_used]
    highway_bias_mine = [
        conv_mine[:, taps_used + 1 + 2 * i : taps_used + 3 + 2 * i].T for i in range(layers)
    ]
    conv_mine = conv_mine[:, :taps_used]
    qkv_mine = jnp.stack([qkvo_mine[:, i * width : (i + 1) * width] for i in range(3)])
    out_mine = qkvo_mine[:, 3 * width :]
    highway_mine = jnp.stack(highway_mine).reshape(layers, 2, per, FILTERS).transpose(0, 3, 1, 2)
    highway_bias_mine = jnp.stack(highway_bias_mine).reshape(layers, 2, per)
    return (
        result.astype(bf16),
        table_grad_t.T[:ids_count],
        conv_mine.T,
        conv_bias_mine,
        highway_mine,
        highway_bias_mine,
        proj_mine,
        proj_bias_grad,
        qkv_mine.transpose(1, 0, 2),
        qv_bias_grad,
        out_mine.T,
        out_bias_grad,
        ln1_gain_grad,
        ln1_bias_grad,
        up_mine,
        up_bias_grad,
        down_mine.T,
        down_bias_grad,
        ln2_gain_grad,
        ln2_bias_grad,
    )


def solution(mesh):
    placed = (
        P(("dp", "tensor"), None),
        P("dp", None),
        P("dp", None, None),
        P(),
        P(None, ("dp", "tensor")),
        P(("dp", "tensor")),
        P(None, None, None, ("dp", "tensor")),
        P(None, None, ("dp", "tensor")),
        P(("dp", "tensor"), None),
        P(),
        P(None, None, "tensor"),
        P(None, "tensor"),
        P("tensor", None),
        P(),
        P(),
        P(),
        P(None, "tensor"),
        P("tensor"),
        P("tensor", None),
        P(),
        P(),
        P(),
    )
    return jax.shard_map(
        per_device,
        mesh=mesh,
        in_specs=placed,
        out_specs=(
            P(("dp", "tensor"), None),
            P(),
            P(None, ("dp", "tensor")),
            P(("dp", "tensor")),
            P(None, None, None, ("dp", "tensor")),
            P(None, None, ("dp", "tensor")),
            P(("dp", "tensor"), None),
            P(),
            P("dp", None, "tensor"),
            P(None, "tensor"),
            P("tensor", "dp"),
            P(),
            P(),
            P(),
            P("dp", "tensor"),
            P("tensor"),
            P("tensor", "dp"),
            P(),
            P(),
            P(),
        ),
        check_vma=False,
    )
```

```python
import functools
import math

import jax
import jax.numpy as jnp
from jax import lax
from jax.experimental import pallas as pl
from jax.experimental.pallas import tpu as pltpu
from jax.sharding import PartitionSpec as P

HEAD_DIM = 64
FILTERS = 2048
CHAR_DIM = 16
CHARS = 50
MAX_WIDTH = 7
LEN = 512
D = 768

channel_shares = (1, 2, 4, 8, 16, 32)
norm_eps = 1e-05
big_negative = -1e30
f32 = jnp.float32
bf16 = jnp.bfloat16
PAIR = "tensor"
GROUP = "dp"
TAPS = 128
VROWS = (CHARS + 7) * CHAR_DIM
FBLOCK = 256


def gelu(x):
    return 0.5 * x * (1.0 + lax.erf(x * (1.0 / math.sqrt(2.0))))


def gelu_both(x):
    share = 0.5 * (1.0 + lax.erf(x * (1.0 / math.sqrt(2.0))))
    return x * share, share + x * jnp.exp(-0.5 * x * x) * (1.0 / math.sqrt(2.0 * math.pi))


def width_of(channel):
    return 1 + sum(channel >= part * (FILTERS // 64) for part in channel_shares)


def dot(a, b, ca, cb):
    return lax.dot_general(a, b, (((ca,), (cb,)), ((), ())), preferred_element_type=f32)


def block_limits(per, start, stop):
    widths = [
        width_of((row // per) * 2 * per + side * per + row % per)
        for row in range(start, stop)
        for side in range(2)
    ]
    return CHARS + 1 - max(widths), CHARS + 1 - min(widths)


MESH = pl.DeviceIdType.MESH
ANYWHERE = pl.BlockSpec(memory_space=pl.ANY)


def pair_swap(x):
    return lax.ppermute(x, PAIR, [(0, 1), (1, 0)])


class Place:
    def __init__(self, lines):
        self.lines = lines
        index = lax.axis_index(GROUP)
        self.side = lax.axis_index(PAIR)
        self.line, self.row, self.core = index // 4, (index // 2) % 2, index % 2
        self.sibling = self.at(self.line, self.row, 1 - self.core)
        self.across = self.at(self.line, 1 - self.row, self.core)
        self.partner = (index, 1 - self.side)

    def at(self, line, row, core):
        return ((line * 2 + row) * 2 + core, self.side)

    def on_line(self, line):
        return self.at(line, self.row, self.core)


def send(source, target, sems, device):
    copy = pltpu.make_async_remote_copy(
        src_ref=source, dst_ref=target, send_sem=sems[0], recv_sem=sems[1],
        device_id=device, device_id_type=MESH,
    )
    copy.start()
    return copy


def meet(devices):
    barrier = pltpu.get_barrier_semaphore()
    for device in devices:
        pl.semaphore_signal(barrier, inc=1, device_id=device, device_id_type=MESH)
    pl.semaphore_wait(barrier, len(devices))


class Gather:
    def __init__(self, place, blocks, wholes, sems):
        self.place, self.blocks, self.wholes = place, blocks, wholes
        self.line_s, self.line_r, self.row_s, self.row_r, self.core_s, self.core_r, self.own = sems

    def piece(self, k, line, row, core):
        return self.wholes[k].at[line, row, core]

    def to_line(self, k, source, line, step):
        p = self.place
        return pltpu.make_async_remote_copy(
            src_ref=source, dst_ref=self.piece(k, line, p.row, p.core),
            send_sem=self.line_s.at[k, line, 0 if step > 0 else 1], recv_sem=self.line_r.at[k, line],
            device_id=p.on_line(lax.rem(p.line + step + p.lines, p.lines)), device_id_type=MESH,
        )

    def to_row(self, k, source, line):
        p = self.place
        return pltpu.make_async_remote_copy(
            src_ref=source, dst_ref=self.piece(k, line, p.row, p.core),
            send_sem=self.row_s.at[k, line], recv_sem=self.row_r.at[k, line],
            device_id=p.across, device_id_type=MESH,
        )

    def to_core(self, k, source, line, row):
        p = self.place
        return pltpu.make_async_remote_copy(
            src_ref=source, dst_ref=self.piece(k, line, row, p.core),
            send_sem=self.core_s.at[k, line, row], recv_sem=self.core_r.at[k, line, row],
            device_id=p.sibling, device_id_type=MESH,
        )

    def pass_on(self, k, line, source, left, right):
        p = self.place
        if right:
            @pl.when(p.line < p.lines - 1)
            def _():
                self.to_line(k, source, line, 1).start()
        if left:
            @pl.when(p.line > 0)
            def _():
                self.to_line(k, source, line, -1).start()
        self.to_row(k, source, line).start()
        self.to_core(k, source, line, p.row).start()

    def begin(self, k):
        p = self.place
        pltpu.make_async_copy(self.blocks[k], self.piece(k, p.line, p.row, p.core), self.own.at[k]).start()
        self.pass_on(k, p.line, self.blocks[k], True, True)

    def from_row(self, k, line):
        p = self.place
        got = self.piece(k, line, 1 - p.row, p.core)
        pltpu.make_async_remote_copy(
            src_ref=got, dst_ref=got, send_sem=self.row_s.at[k, line], recv_sem=self.row_r.at[k, line],
            device_id=p.across, device_id_type=MESH,
        ).wait_recv()
        self.to_core(k, got, line, 1 - p.row).start()

    def turn(self, k, r):
        p = self.place
        for step in (1, -1):
            line = p.line - step * r
            inside = (line >= 0) & (line < p.lines)

            @pl.when(inside)
            def _(line=line, step=step):
                got = self.piece(k, line, p.row, p.core)
                self.to_line(k, got, line, step).wait_recv()
                self.pass_on(k, line, got, step < 0, step > 0)
        self.crossed(k, r - 1)

    def crossed(self, k, r):
        p = self.place
        for step in (1, -1) if r else (1,):
            line = p.line - step * r
            inside = (line >= 0) & (line < p.lines)

            @pl.when(inside)
            def _(line=line):
                self.from_row(k, line)

    def finish(self, k):
        p = self.place
        self.crossed(k, p.lines - 1)
        own = self.piece(k, p.line, p.row, p.core)
        pltpu.make_async_copy(self.blocks[k], own, self.own.at[k]).wait()

        def each(line, carry):
            for row in range(2):
                self.to_core(k, self.piece(k, line, row, p.core), line, row).wait_send()
                self.to_core(k, self.piece(k, line, row, 1 - p.core), line, row).wait_recv()
            self.to_row(k, self.piece(k, line, p.row, p.core), line).wait_send()

            @pl.when((p.line < p.lines - 1) & (line <= p.line))
            def _():
                self.to_line(k, self.piece(k, line, p.row, p.core), line, 1).wait_send()

            @pl.when((p.line > 0) & (line >= p.line))
            def _():
                self.to_line(k, self.piece(k, line, p.row, p.core), line, -1).wait_send()
            return carry

        lax.fori_loop(0, p.lines, each, 0)

    @staticmethod
    def sems(count, lines):
        dma = pltpu.SemaphoreType.DMA
        return [
            dma((count, lines, 2)), dma((count, lines)), dma((count, lines)), dma((count, lines)),
            dma((count, lines, 2)), dma((count, lines, 2)), dma((count,)),
        ]


def neighbours(place, partner):
    others = [
        place.on_line(lax.rem(place.line + step, place.lines)) for step in range(1, place.lines)
    ]
    return [place.sibling, place.across, *others] + ([place.partner] if partner else [])


def gather_kernel(lines, count, swap, *refs):
    blocks, refs = refs[:count], refs[count:]
    swap_in, refs = refs[:swap], refs[swap:]
    wholes, refs = refs[:count], refs[count:]
    swap_out, refs = refs[:swap], refs[swap:]
    place = Place(lines)
    gather = Gather(place, blocks, wholes, refs[:7])
    meet(neighbours(place, bool(swap)))
    for k in range(count):
        gather.begin(k)
    if swap:
        copy = send(swap_in[0], swap_out[0], refs[7:9], place.partner)
    for r in range(1, lines):
        for k in range(count):
            gather.turn(k, r)
    for k in range(count):
        gather.finish(k)
    if swap:
        copy.wait()


def gather_blocks(blocks, lines, ident, swap=None):
    count = len(blocks)
    swaps = [] if swap is None else [swap]
    dma = pltpu.SemaphoreType.DMA
    outs = pl.pallas_call(
        functools.partial(gather_kernel, lines, count, len(swaps)),
        out_shape=tuple(
            [jax.ShapeDtypeStruct((lines, 2, 2) + b.shape, b.dtype) for b in blocks]
            + [jax.ShapeDtypeStruct(s.shape, s.dtype) for s in swaps]
        ),
        in_specs=[ANYWHERE] * (count + len(swaps)),
        out_specs=tuple([ANYWHERE] * (count + len(swaps))),
        scratch_shapes=Gather.sems(count, lines) + [dma, dma] * len(swaps),
        compiler_params=pltpu.CompilerParams(collective_id=ident, has_side_effects=True),
    )(*blocks, *swaps)
    return [o.reshape((4 * lines,) + b.shape) for o, b in zip(outs, blocks)] + list(outs[count:])


class Scatter:
    def __init__(self, place, arrays, from_core, from_row, from_line, outs, pieces, bufs, sems):
        self.place, self.arrays, self.outs, self.pieces = place, arrays, outs, pieces
        self.from_core, self.from_row, self.from_line = from_core, from_row, from_line
        self.mine, self.theirs, self.sums, self.crossed, self.leaving, self.arrived = bufs
        self.core_s, self.core_r, self.row_s, self.row_r, self.line_s, self.line_r, self.load = sems

    def span(self, k):
        array, start, size = self.pieces[k]
        return array, pl.ds(start, size), size, self.arrays[array].shape[-1]

    def core_copy(self, k):
        array, rows, size, width = self.span(k)
        p = self.place
        return pltpu.make_async_remote_copy(
            src_ref=self.arrays[array].at[:, :, 1 - p.core, rows],
            dst_ref=self.from_core[array].at[:, :, rows],
            send_sem=self.core_s.at[k], recv_sem=self.core_r.at[k],
            device_id=p.sibling, device_id_type=MESH,
        )

    def row_copy(self, k):
        array, rows, size, width = self.span(k)
        p = self.place
        return pltpu.make_async_remote_copy(
            src_ref=self.sums.at[k % self.sums.shape[0], 1 - p.row, :, pl.ds(0, size), pl.ds(0, width)],
            dst_ref=self.from_row[array].at[:, rows],
            send_sem=self.row_s.at[k], recv_sem=self.row_r.at[k],
            device_id=p.across, device_id_type=MESH,
        )

    def line_copy(self, k, step):
        array, rows, size, width = self.span(k)
        p = self.place
        line = lax.rem(p.line + step, p.lines)
        return pltpu.make_async_remote_copy(
            src_ref=self.leaving.at[k % self.leaving.shape[0], line, pl.ds(0, size), pl.ds(0, width)],
            dst_ref=self.from_line[array].at[step, rows],
            send_sem=self.line_s.at[k, step], recv_sem=self.line_r.at[k, step],
            device_id=p.on_line(line), device_id_type=MESH,
        )

    def begin(self, k):
        self.core_copy(k).start()

    def add_core(self, k):
        array, rows, size, width = self.span(k)
        p = self.place
        slot = k % self.sums.shape[0]
        if k >= self.sums.shape[0]:
            self.row_copy(k - self.sums.shape[0]).wait_send()
        here = (slice(None), slice(None), pl.ds(0, size), pl.ds(0, width))
        mine = pltpu.make_async_copy(
            self.arrays[array].at[:, :, p.core, rows], self.mine.at[here], self.load.at[0]
        )
        mine.start()
        self.core_copy(k).wait_recv()
        theirs = pltpu.make_async_copy(
            self.from_core[array].at[:, :, rows], self.theirs.at[here], self.load.at[1]
        )
        theirs.start()
        mine.wait()
        theirs.wait()

        def each(i, carry):
            line = i // (size // 16)
            part = pl.ds(pl.multiple_of((i % (size // 16)) * 16, 16), 16)
            for row in range(2):
                total = self.mine[line, row, part, :width].astype(f32) + self.theirs[
                    line, row, part, :width
                ].astype(f32)
                self.sums[slot, row, line, part, :width] = total.astype(bf16)
            return carry

        lax.fori_loop(0, p.lines * (size // 16), each, 0)
        self.row_copy(k).start()

    def add_row(self, k):
        array, rows, size, width = self.span(k)
        p = self.place
        slot = k % self.sums.shape[0]
        away = k % self.leaving.shape[0]
        if k >= self.leaving.shape[0]:
            for step in range(1, p.lines):
                self.line_copy(k - self.leaving.shape[0], step).wait_send()
        here = (slice(None), pl.ds(0, size), pl.ds(0, width))
        self.row_copy(k).wait_recv()
        copy = pltpu.make_async_copy(
            self.from_row[array].at[:, rows], self.crossed.at[here], self.load.at[2]
        )
        copy.start()
        copy.wait()

        def each(i, carry):
            line = i // (size // 16)
            part = pl.ds(pl.multiple_of((i % (size // 16)) * 16, 16), 16)
            total = self.sums[slot, p.row, line, part, :width].astype(f32) + self.crossed[
                line, part, :width
            ].astype(f32)
            self.leaving[away, line, part, :width] = total.astype(bf16)
            return carry

        lax.fori_loop(0, p.lines * (size // 16), each, 0)
        for step in range(1, p.lines):
            self.line_copy(k, step).start()
        own = self.leaving.at[away, p.line, pl.ds(0, size), pl.ds(0, width)]
        copy = pltpu.make_async_copy(own, self.from_line[array].at[0, rows], self.load.at[3])
        copy.start()
        copy.wait()

    def add_line(self, k):
        array, rows, size, width = self.span(k)
        start = self.pieces[k][1]
        p = self.place
        for step in range(1, p.lines):
            self.line_copy(k, step).wait_recv()
        here = (slice(None), pl.ds(0, size), pl.ds(0, width))
        copy = pltpu.make_async_copy(
            self.from_line[array].at[:, rows], self.arrived.at[here], self.load.at[4]
        )
        copy.start()
        copy.wait()

        def each(i, carry):
            part = pl.ds(pl.multiple_of(i * 16, 16), 16)
            total = self.arrived[0, part, :width].astype(f32)
            for step in range(1, p.lines):
                total = total + self.arrived[step, part, :width].astype(f32)
            self.outs[array][pl.ds(pl.multiple_of(start + i * 16, 16), 16), :] = total
            return carry

        lax.fori_loop(0, size // 16, each, 0)

    def order(self, count):
        work = []
        lead = self.sums.shape[0] - 1
        for k in range(count + lead + 2):
            if k < count:
                work.append(("add_core", k))
            if 0 <= k - lead < count:
                work.append(("add_row", k - lead))
            if 0 <= k - lead - 2 < count:
                work.append(("add_line", k - lead - 2))
        return work

    def finish(self):
        count = len(self.pieces)
        for k in range(count):
            self.core_copy(k).wait_send()
            if k >= count - self.sums.shape[0]:
                self.row_copy(k).wait_send()
            if k >= count - self.leaving.shape[0]:
                for step in range(1, self.place.lines):
                    self.line_copy(k, step).wait_send()

    @staticmethod
    def shapes(arrays, pieces, lines):
        land = []
        for lead in ((lines, 2), (lines,), (lines,)):
            land += [jax.ShapeDtypeStruct(lead + a.shape[3:], bf16) for a in arrays]
        outs = [jax.ShapeDtypeStruct(a.shape[3:], f32) for a in arrays]
        rows = max(size for _, _, size in pieces)
        width = max(a.shape[-1] for a in arrays)
        dma = pltpu.SemaphoreType.DMA
        count = len(pieces)
        slots = 4 if lines <= 8 else 2
        bufs = [
            pltpu.VMEM((lines, 2, rows, width), bf16), pltpu.VMEM((lines, 2, rows, width), bf16),
            pltpu.VMEM((slots, 2, lines, rows, width), bf16), pltpu.VMEM((lines, rows, width), bf16),
            pltpu.VMEM((slots // 2, lines, rows, width), bf16), pltpu.VMEM((lines, rows, width), bf16),
        ]
        sems = [dma((count,))] * 4 + [dma((count, lines))] * 2 + [dma((5,))]
        return land, outs, bufs, sems


def cut(arrays, most):
    pieces = []
    for i, a in enumerate(arrays):
        rows = a.shape[3]
        size = max(s for s in range(16, most + 1, 16) if rows % s == 0)
        pieces += [(i, start, size) for start in range(0, rows, size)]
    return pieces


def onehot_chars(ids_row, count):
    return jnp.where(
        lax.broadcasted_iota(jnp.int32, (count, ids_row.shape[1]), 0) == ids_row, 1.0, 0.0
    ).astype(bf16)


class Pooling:
    group = 32

    def __init__(self, limits, chars, weight, lim, pooled, bufs):
        self.limits, self.chars, self.weight, self.lim = limits, chars, weight, lim
        self.pooled, self.bufs = pooled, bufs
        self.halves = chars.shape[1] // FBLOCK
        self.units = [(b, h) for b in range(len(limits)) for h in range(self.halves)]

    def convolve(self, u, p):
        block, half = self.units[u]
        rows = pl.ds(pl.multiple_of(p * CHAR_DIM, CHAR_DIM), TAPS)
        taps = self.chars[rows, pl.ds(half * FBLOCK, FBLOCK)]
        self.bufs[u % 2][p] = dot(self.weight[pl.ds(block * FBLOCK, FBLOCK), :], taps, 1, 0)

    def pool(self, u, g):
        block, half = self.units[u]
        full, some = self.limits[block]
        buf, size = self.bufs[u % 2], self.group
        here = pl.ds(pl.multiple_of(g * size, size), size)
        there = pl.ds(pl.multiple_of(block * FBLOCK + g * size, size), size)
        lim = self.lim[there, :] if some > full else None

        def entry(p):
            value = buf[p, here, :]
            return value if p < full else jnp.where(lim[:, :1] >= p, value, big_negative)

        top = entry(0)
        for p in range(1, some):
            top = jnp.maximum(top, entry(p))
        total = jnp.exp(entry(0) - top)
        for p in range(1, some):
            total = total + jnp.exp(entry(p) - top)
        self.pooled[there, pl.ds(half * FBLOCK, FBLOCK)] = top + jnp.log(total)

    def step(self, u):
        count = FBLOCK // self.group
        todo = self.limits[self.units[u][0]][1] if u < len(self.units) else 0
        each = -(-todo // count)

        def body(g, carry):
            for i in range(each):
                self.convolve(u, jnp.minimum(g * each + i, todo - 1))
            if u:
                self.pool(u - 1, g)
            return carry

        lax.fori_loop(0, count, body, 0)


def embed_kernel(
    lines, limits, ids_ref, table_ref, lim_ref, packed_ref, highway_ref,
    packed_all, highway_all, ids_all, chars_ref, weight_ref, pooled_ref, state_ref, low_ref, other_ref,
    buf_a, buf_b, packed_vmem, ids_s, ids_r, load, state_s, state_r, *sems,
):
    place = Place(lines)
    half = highway_ref.shape[0] // 2
    gather = Gather(
        place,
        [packed_ref] + [highway_ref.at[pl.ds(i * half, half)] for i in range(2)],
        [packed_all] + [highway_all.at[:, :, :, pl.ds(i * half, half)] for i in range(2)],
        sems,
    )
    meet(neighbours(place, True))
    gather.begin(0)
    ids_copy = send(ids_ref, ids_all.at[place.side], (ids_s, ids_r), place.partner)
    own_copy = pltpu.make_async_copy(ids_ref, ids_all.at[place.side], load)
    own_copy.start()
    gather.begin(1)
    gather.begin(2)
    own_copy.wait()
    ids_copy.wait()
    count = ids_ref.shape[0]

    def embed(c, carry):
        for i in range(5):
            row = pl.ds(c * 5 + i, 1)
            ids = jnp.concatenate([ids_all[0, row, :], ids_all[1, row, :]], axis=1)
            hot = onehot_chars(ids, table_ref.shape[1])
            rows = pl.ds(pl.multiple_of((c * 5 + i) * CHAR_DIM, CHAR_DIM), CHAR_DIM)
            chars_ref[rows, :] = dot(table_ref[...], hot, 1, 0).astype(bf16)
        return carry

    lax.fori_loop(0, count // 5, embed, 0)
    words = chars_ref.shape[1]
    chars_ref[CHARS * CHAR_DIM :, :] = jnp.zeros((VROWS - CHARS * CHAR_DIM, words), bf16)
    for r in range(1, lines):
        gather.turn(0, r)
    gather.finish(0)
    copy = pltpu.make_async_copy(packed_all, packed_vmem, load)
    copy.start()
    copy.wait()
    rows = weight_ref.shape[0]
    packed = packed_vmem[...].reshape(rows, TAPS)
    shift = lax.broadcasted_iota(jnp.int32, (rows, TAPS), 1)
    keep = (shift < (CHARS - lim_ref[...]) * CHAR_DIM) & (shift < MAX_WIDTH * CHAR_DIM)
    weight_ref[...] = jnp.where(keep, packed, 0.0).astype(bf16)
    gather.turn(1, 1)
    gather.turn(2, 1)

    pooling = Pooling(limits, chars_ref, weight_ref, lim_ref, pooled_ref, (buf_a, buf_b))
    steps = len(pooling.units) + 1
    copies = []
    due = {max(1, (steps * r) // lines): r for r in range(2, lines)} if lines <= steps else {}
    for u in range(steps):
        pooling.step(u)
        done = u - 1
        if done >= 0 and done % pooling.halves == pooling.halves - 1:
            block = done // pooling.halves
            span = pl.ds(block * FBLOCK, FBLOCK)
            bias = packed_vmem[...].reshape(rows, TAPS)[block * FBLOCK : (block + 1) * FBLOCK, 112:113]
            state = gelu(pooled_ref[span, :] + bias)
            state_ref[span, :] = state
            low_ref[span, :] = state.astype(bf16)
            copies.append(
                send(
                    low_ref.at[span], other_ref.at[span], (state_s.at[block], state_r.at[block]),
                    place.partner,
                )
            )
        if u in due:
            for k in (1, 2):
                gather.turn(k, due[u])
    for r in range(2, lines):
        if r not in due.values():
            for k in (1, 2):
                gather.turn(k, r)
    for k in (1, 2):
        gather.finish(k)
    for copy in copies:
        copy.wait()


def embed_words(ids, table, lim, packed, highway, lines, per, ident):
    own = lim.shape[0]
    words = 2 * ids.shape[1]
    limits = tuple(block_limits(per, s, s + FBLOCK) for s in range(0, own, FBLOCK))
    dma = pltpu.SemaphoreType.DMA
    vmem = pl.BlockSpec(memory_space=pltpu.VMEM)
    blocks = len(limits)
    shape = jax.ShapeDtypeStruct
    return pl.pallas_call(
        functools.partial(embed_kernel, lines, limits),
        out_shape=(
            shape((lines, 2, 2) + packed.shape, f32),
            shape((lines, 2, 2) + highway.shape, bf16),
            shape((2,) + ids.shape, jnp.int32),
            shape((VROWS, words), bf16),
            shape((own, TAPS), bf16),
            shape((own, words), f32),
            shape((own, words), f32),
            shape((own, words), bf16),
            shape((own, words), bf16),
        ),
        in_specs=[vmem, vmem, vmem, ANYWHERE, ANYWHERE],
        out_specs=(ANYWHERE, ANYWHERE, vmem, vmem, vmem, vmem, vmem, vmem, ANYWHERE),
        scratch_shapes=[
            pltpu.VMEM((CHARS, FBLOCK, FBLOCK), f32), pltpu.VMEM((CHARS, FBLOCK, FBLOCK), f32),
            pltpu.VMEM((lines, 2, 2) + packed.shape, f32), dma, dma, dma, dma((blocks,)), dma((blocks,)),
            *Gather.sems(3, lines),
        ],
        compiler_params=pltpu.CompilerParams(
            collective_id=ident, has_side_effects=True, vmem_limit_bytes=56 << 20
        ),
    )(ids, table, lim, packed, highway)


LANE = 128
TABLE_ROWS = 48
HEAD_ROWS = 56


class Totals:
    def __init__(self, place, value, inbox, send_sems, recv_sems):
        self.place, self.value, self.inbox = place, value, inbox
        self.send_sems, self.recv_sems = send_sems, recv_sems
        self.partners = [place.sibling, place.across]
        span = 1
        while span < place.lines:
            low = lax.rem(place.line // span, 2)
            self.partners.append(place.on_line(place.line + span - 2 * span * low))
            span *= 2
        self.partners.append(place.partner)

    def start(self, i):
        self.copy = send(
            self.value, self.inbox.at[i], (self.send_sems.at[i], self.recv_sems.at[i]), self.partners[i]
        )

    def end(self, i):
        self.copy.wait()
        self.value[...] = self.value[...] + self.inbox[i]


def bias_lane(rows, lane, value):
    return jnp.where(lax.broadcasted_iota(jnp.int32, (rows, LANE), 1) == lane, value, 0.0)


def back_kernel(lines, limits, per, pieces, taps_used, *refs):
    refs = iter(refs)

    def take(n):
        return [next(refs) for _ in range(n)]

    enc = take(3)
    (de_ref, base_ref, proj_ref, low_ref, packed_ref, conv_ref, conv_t_ref, lim_ref, ids_ref, vec_in) = take(10)
    kept_hbm = [take(5), take(5)]
    pooled_hbm, chars_hbm = take(2)
    land = take(3 * 7)
    highway_hbm = take(2)
    outs = take(7)
    (vec_ref,) = take(1)
    scatter_bufs, scatter_sems = take(6), take(7)
    (kst, knl, kgt, full, wbuf, acc, dpre, dpre_t, gs) = take(9)
    (demb, leave, come, projg, convg, pack, dchars, chars, inbox) = take(9)
    (load_s, weight_s, out_s, swap_s, swap_r, total_s, total_r) = take(7)

    place = Place(lines)
    side = place.side
    arrays = [*enc, projg, highway_hbm[1], highway_hbm[0], convg]
    scatter = Scatter(
        place, arrays, land[:7], land[7:14], land[14:], outs, pieces, scatter_bufs, scatter_sems
    )
    of_array = [[k for k, piece in enumerate(pieces) if piece[0] == i] for i in range(7)]
    main = of_array[6][0]
    ticks = scatter.order(main)
    meet(neighbours(place, True))

    def go(kind, k):
        while (kind, k) in ticks:
            tick = ticks.pop(0)
            getattr(scatter, tick[0])(tick[1])

    def begin(i):
        for k in of_array[i]:
            scatter.begin(k)

    own, words = gs.shape
    quarter = own // 4
    lines_each = lines // 4

    def loads(layer):
        state, nonlin, gate, both, _ = kept_hbm[layer]
        copies = [
            pltpu.make_async_copy(src, dst, load_s.at[i])
            for i, (src, dst) in enumerate(((state, kst), (nonlin, knl), (gate, kgt), (both, full)))
        ]
        for copy in copies:
            copy.start()
        return copies

    def weights(layer, q):
        copy = pltpu.make_async_copy(
            kept_hbm[layer][4].at[pl.ds(q * lines_each, lines_each)], wbuf.at[q % 2], weight_s.at[q % 2]
        )
        copy.start()
        return copy

    kept_copies = loads(1)
    weight_copies = [weights(1, 0), weights(1, 1)]
    de_copy = send(de_ref, demb, (swap_s.at[2], swap_r.at[2]), place.partner)
    for i in range(3):
        begin(i)
    vec_ref[...] = vec_in[...]
    pack[...] = jnp.zeros_like(pack)
    go("add_core", 2)
    de_copy.wait()

    total = jnp.zeros((1, demb.shape[1]), f32)
    for c in range(words // LANE):
        rows = pl.ds(c * LANE, LANE)
        value = (base_ref[rows, :] + demb[rows, :].astype(f32)).astype(bf16)
        demb[rows, :] = value
        total = total + jnp.sum(value.astype(f32), axis=0, keepdims=True)
    total = jnp.where(side == 0, total, 0.0)
    for j in range(demb.shape[1] // LANE):
        vec_ref[TABLE_ROWS + j : TABLE_ROWS + j + 1, :] = total[:, j * LANE : (j + 1) * LANE]

    def project(c, carry):
        rows = pl.ds(pl.multiple_of(c * LANE, LANE), LANE)
        grad = dot(low_ref[rows, :], demb[...], 1, 0)
        for j in range(LANE // per):
            index = c * (LANE // per) + j
            projg[index // 4, (index // 2) % 2, index % 2, :per, :] = grad[j * per : (j + 1) * per].astype(bf16)
        gs[rows, :] = dot(proj_ref[rows, :], demb[...], 1, 1)
        return carry

    lax.fori_loop(0, own // LANE, project, 0)
    begin(3)
    go("add_row", 0)

    def layer(l, marks):
        for copy in kept_copies:
            copy.wait()

        def slopes(c, carry):
            rows = pl.ds(pl.multiple_of(c * 64, 64), 64)
            grad, nonlin, gate = gs[rows, :], knl[rows, :], kgt[rows, :]
            through = grad * (1.0 - gate)
            value, slope = gelu_both(nonlin)
            d_nonlin = through * slope
            d_gate = grad * (kst[rows, :] - value) * gate * (1.0 - gate)
            gs[rows, :] = grad * gate
            both = jnp.stack(
                [d_nonlin.reshape(64 // per, per, words), d_gate.reshape(64 // per, per, words)], axis=1
            ).reshape(128, words)
            dpre[pl.ds(pl.multiple_of(c * 128, 128), 128), :] = both.astype(bf16)
            dpre_t[:, pl.ds(pl.multiple_of(c * 128, 128), 128)] = both.T.astype(bf16)
            at = taps_used + 1 + 2 * l
            pack[rows, :] += bias_lane(64, at, jnp.sum(d_nonlin, axis=1, keepdims=True)) + bias_lane(
                64, at + 1, jnp.sum(d_gate, axis=1, keepdims=True)
            )
            return carry

        lax.fori_loop(0, own // 64, slopes, 0)
        for q in range(4):
            weight_copies[q % 2].wait()

            def back(n, carry, q=q):
                lanes = pl.ds(pl.multiple_of(n * 256, 256), 256)
                matrix = wbuf[q % 2, :, :, :, :, lanes].reshape(2 * quarter, 256)
                part = dot(dpre_t[:, 2 * quarter * q : 2 * quarter * (q + 1)], matrix, 1, 0)
                if q:
                    part = acc[:, lanes] + part
                acc[:, lanes] = part
                return carry

            lax.fori_loop(0, FILTERS // 256, back, 0)
            if q < 2:
                weight_copies[q % 2] = weights(l, q + 2)
            if marks[q]:
                go(*marks[q])

        def turn(c, carry):
            part = acc[:, pl.ds(pl.multiple_of(c * 128, 128), 128)].T.reshape(64 // per, 2, per, words)
            first, second = part[:, 0].reshape(64, words), part[:, 1].reshape(64, words)
            rows = pl.ds(pl.multiple_of(c * 64, 64), 64)
            gs[rows, :] += jnp.where(side == 0, first, second)
            leave[rows, :] = jnp.where(side == 0, second, first).astype(bf16)
            return carry

        lax.fori_loop(0, own // 64, turn, 0)
        swap = send(leave, come.at[l], (swap_s.at[l], swap_r.at[l]), place.partner)
        stores = [None, None]
        for q in range(4):
            if stores[q % 2] is not None:
                stores[q % 2].wait()

            def grads(n, carry, q=q):
                lanes = pl.ds(pl.multiple_of(n * 256, 256), 256)
                part = dot(dpre[2 * quarter * q : 2 * quarter * (q + 1), :], full[lanes, :], 1, 1)
                wbuf[q % 2, :, :, :, :, lanes] = part.astype(bf16).reshape(
                    lines_each, 2, 2, 2 * per, 256
                )
                return carry

            lax.fori_loop(0, FILTERS // 256, grads, 0)
            stores[q % 2] = pltpu.make_async_copy(
                wbuf.at[q % 2], highway_hbm[l].at[pl.ds(q * lines_each, lines_each)], out_s.at[q % 2]
            )
            stores[q % 2].start()
            if marks[4 + q]:
                go(*marks[4 + q])
        for store in stores:
            store.wait()
        return swap

    def arrive(l, swap):
        swap.wait()

        def add(c, carry):
            rows = pl.ds(pl.multiple_of(c * 64, 64), 64)
            gs[rows, :] += come[l, rows, :].astype(f32)
            return carry

        lax.fori_loop(0, own // 64, add, 0)

    first_hw = [of_array[4][0], of_array[5][0]]
    swap = layer(1, [None, ("add_core", first_hw[0] - 1), None, ("add_row", 1)] + [None] * 4)
    kept_copies = loads(0)
    weight_copies = [weights(0, 0), weights(0, 1)]
    begin(4)
    go("add_core", first_hw[1] - 1)
    arrive(1, swap)
    swap = layer(0, [None] * 8)
    begin(5)
    copies = [
        pltpu.make_async_copy(pooled_hbm, kst, load_s.at[0]),
        pltpu.make_async_copy(chars_hbm, chars, load_s.at[3]),
    ]
    for copy in copies:
        copy.start()
    go("add_core", first_hw[1] + 1)
    arrive(0, swap)
    for copy in copies:
        copy.wait()

    def pooled_grad(c, carry):
        rows = pl.ds(pl.multiple_of(c * 64, 64), 64)
        _, slope = gelu_both(kst[rows, :] + packed_ref[rows, taps_used : taps_used + 1])
        grad = gs[rows, :] * slope
        gs[rows, :] = grad
        pack[rows, :] += bias_lane(64, taps_used, jnp.sum(grad, axis=1, keepdims=True))
        return carry

    lax.fori_loop(0, own // 64, pooled_grad, 0)
    dchars[...] = jnp.zeros_like(dchars)
    wgrad = knl.at[:, :TAPS]
    wgrad[...] = jnp.zeros((own, TAPS), f32)
    slots = [dpre.at[:own], dpre.at[own:], full.at[:own], full.at[own:]]

    def place_at(p, blocks, slot):
        window = pl.ds(p * CHAR_DIM if isinstance(p, int) else pl.multiple_of(p * CHAR_DIM, CHAR_DIM), TAPS)
        taps = chars[window, :]
        dconv = slots[slot]
        for block in range(blocks):
            full_places, _ = limits[block]
            rows = pl.ds(block * FBLOCK, FBLOCK)
            value = jnp.exp(dot(conv_ref[rows, :], taps, 1, 0) - kst[rows, :]) * gs[rows, :]
            if isinstance(p, int) and p >= full_places:
                value = jnp.where(lim_ref[rows, :][:, :1] >= p, value, 0.0)
            dconv[rows, :] = value.astype(bf16)
        rows = pl.ds(0, blocks * FBLOCK)
        wgrad[rows, :] += dot(dconv[rows, :], taps, 1, 1)
        dchars[window, :] += dot(conv_t_ref[:, : blocks * FBLOCK], dconv[rows, :], 1, 0)

    always = min(full_places for full_places, _ in limits)
    ever = max(some for _, some in limits)
    stretches = 11
    runs = -(-(always // 4) // stretches)
    left = len(ticks)
    done = 0
    for s in range(stretches):
        start, stop = s * runs, min((s + 1) * runs, always // 4)

        def four(i, carry):
            for u in range(4):
                place_at(i * 4 + u, len(limits), u)
            return carry

        lax.fori_loop(start, stop, four, 0)
        while done < left * (s + 1) // (stretches + 2):
            getattr(scatter, ticks[0][0])(ticks[0][1])
            ticks.pop(0)
            done += 1
    for p in range(always // 4 * 4, ever):
        blocks = 1 + max(block for block, (_, some) in enumerate(limits) if p < some)
        place_at(p, blocks, p % 4)
    lane = lax.broadcasted_iota(jnp.int32, (own, TAPS), 1)
    keep = (lane < (CHARS - lim_ref[...]) * CHAR_DIM) & (lane < taps_used)
    result = (pack[...] + jnp.where(keep, wgrad[...], 0.0)).astype(bf16)
    convg[:, :, :, :per, :] = result.reshape(lines, 2, 2, per, LANE)
    begin(6)

    ids_count = TABLE_ROWS // CHAR_DIM * LANE

    def spread(c, total):
        for i in range(5):
            rows = pl.ds(pl.multiple_of((c * 5 + i) * CHAR_DIM, CHAR_DIM), CHAR_DIM)
            row = pl.ds(c * 5 + i, 1)
            ids = jnp.concatenate([ids_ref[0, row, :], ids_ref[1, row, :]], axis=1)
            total = total + dot(dchars[rows, :].astype(bf16), onehot_chars(ids, ids_count), 1, 1)
        return total

    table = lax.fori_loop(0, CHARS // 5, spread, jnp.zeros((CHAR_DIM, ids_count), f32))
    for j in range(ids_count // LANE):
        vec_ref[j * CHAR_DIM : (j + 1) * CHAR_DIM, :] = table[:, j * LANE : (j + 1) * LANE]
    totals = Totals(place, vec_ref, inbox, total_s, total_r)
    while ticks:
        getattr(scatter, ticks[0][0])(ticks[0][1])
        ticks.pop(0)
    last = of_array[6]
    phases = [scatter.add_core, scatter.add_row, scatter.add_line]
    for i in range(len(totals.partners)):
        totals.start(i)
        if i < 3:
            for k in last:
                phases[i](k)
        totals.end(i)
    scatter.finish()


def embedder_backward(
    enc, de_low, base, proj_all, low, packed, conv, lim, ids, vec, kept, pooled, chars, lines, per,
    taps_used, ident,
):
    own, words = low.shape
    limits = tuple(block_limits(per, s, s + FBLOCK) for s in range(0, own, FBLOCK))
    shape = jax.ShapeDtypeStruct
    tall = max(per, 16)
    whole = []
    for a in enc:
        rows = -(-a.shape[1] // 16) * 16
        a = jnp.pad(a, ((0, 0), (0, rows - a.shape[1]), (0, 0)))
        whole.append(a.reshape((lines, 2, 2) + a.shape[1:]))
    lead = (lines, 2, 2)
    width = proj_all.shape[1]
    made = [
        shape(lead + (tall, width), bf16),
        shape(lead + (2 * per, FILTERS), bf16),
        shape(lead + (2 * per, FILTERS), bf16),
        shape(lead + (tall, LANE), bf16),
    ]
    arrays = whole + made
    pieces = cut(arrays, 48)
    land, outs, bufs, sems = Scatter.shapes(arrays, pieces, lines)
    dma = pltpu.SemaphoreType.DMA
    vmem = pl.BlockSpec(memory_space=pltpu.VMEM)
    steps = 3 + (lines - 1).bit_length()
    layers = [
        (state, nonlin, gate, both, weight.reshape(lead + (2 * per, FILTERS)))
        for state, nonlin, gate, both, weight in kept
    ]
    result = pl.pallas_call(
        functools.partial(back_kernel, lines, limits, per, pieces, taps_used),
        out_shape=tuple(land + [made[1], made[1]] + outs + [shape(vec.shape, f32)]),
        in_specs=[ANYWHERE] * 4 + [vmem] * 9 + [ANYWHERE] * 12,
        out_specs=tuple([ANYWHERE] * (len(land) + 2) + [vmem] * (len(outs) + 1)),
        scratch_shapes=bufs
        + sems
        + [
            pltpu.VMEM((own, words), f32), pltpu.VMEM((own, words), f32), pltpu.VMEM((own, words), f32),
            pltpu.VMEM((2 * own, words), bf16),
            pltpu.VMEM((2, lines // 4, 2, 2, 2 * per, FILTERS), bf16),
            pltpu.VMEM((words, FILTERS), f32),
            pltpu.VMEM((2 * own, words), bf16), pltpu.VMEM((words, 2 * own), bf16),
            pltpu.VMEM((own, words), f32), pltpu.VMEM((words, width), bf16),
            pltpu.VMEM((own, words), bf16),
            pltpu.VMEM((2, own, words), bf16),
            pltpu.VMEM(made[0].shape, bf16), pltpu.VMEM(made[3].shape, bf16),
            pltpu.VMEM((own, LANE), f32), pltpu.VMEM((VROWS, words), f32), pltpu.VMEM((VROWS, words), bf16),
            pltpu.VMEM((steps,) + vec.shape, f32),
            dma((4,)), dma((2,)), dma((2,)), dma((3,)), dma((3,)), dma((steps,)), dma((steps,)),
        ],
        compiler_params=pltpu.CompilerParams(
            collective_id=ident, has_side_effects=True, vmem_limit_bytes=62 << 20
        ),
    )(
        *whole, de_low, base, proj_all, low, packed, conv, conv.T, lim, ids, vec,
        *layers[0], *layers[1], pooled, chars,
    )
    outs = result[len(land) + 2 : -1]
    heights = [a.shape[1] for a in enc] + [per, 2 * per, 2 * per, per]
    return [o[:h] for o, h in zip(outs, heights)], result[-1]


def norm_forward(summed):
    centred = summed - jnp.mean(summed, axis=-1, keepdims=True)
    inv_std = lax.rsqrt(jnp.mean(centred * centred, axis=-1, keepdims=True) + norm_eps)
    return centred * inv_std, inv_std


def norm_backward(grad_out, normalized, inv_std, gain):
    grad_norm = grad_out * gain
    return inv_std * (
        grad_norm
        - jnp.mean(grad_norm, axis=-1, keepdims=True)
        - normalized * jnp.mean(grad_norm * normalized, axis=-1, keepdims=True)
    )


def split_two(x):
    high = x.astype(bf16)
    return high, (x - high.astype(f32)).astype(bf16)


def per_device(
    char_ids, mask_pos, out_grad, char_table, conv_weight, conv_bias, highway_weight, highway_bias,
    proj_weight, proj_bias, qkv_weight, qv_bias, out_weight, out_bias, ln1_gain, ln1_bias, up_weight,
    up_bias, down_weight, down_bias, ln2_gain, ln2_bias,
):
    side = lax.axis_index(PAIR)
    per = conv_weight.shape[1]
    ndp = FILTERS // (2 * per)
    rows_here = char_ids.shape[0]
    words = 2 * rows_here
    own = ndp * per
    layers = highway_weight.shape[0]
    ids_count = char_table.shape[0]
    padded_ids = -(-ids_count // 128) * 128

    taps_used = conv_weight.shape[0]
    packed = jnp.concatenate(
        [
            conv_weight.T.astype(f32),
            conv_bias[:, None].astype(f32),
            highway_bias.reshape(2 * layers, per).T.astype(f32),
            jnp.zeros((per, TAPS - taps_used - 1 - 2 * layers), f32),
        ],
        axis=1,
    )
    highway_t = highway_weight.transpose(0, 2, 3, 1)
    lines = ndp // 4
    blocks = [highway_t[i].reshape(2 * per, FILTERS) for i in range(layers)]
    highway_all = [None] * layers

    filter_index = jnp.arange(own, dtype=jnp.int32)
    filter_index = (filter_index // per) * (2 * per) + side * per + filter_index % per
    filter_width = width_of(filter_index).astype(jnp.int32)
    lim = jnp.broadcast_to((CHARS - filter_width)[:, None], (own, 128))
    table_t = jnp.pad(char_table.T, ((0, 0), (0, padded_ids - ids_count)))
    (
        packed_all, highway_all[0], ids, chars, conv_all, pooled_raw, state, state_low, other_low,
    ) = embed_words(char_ids.T, table_t, lim, packed, blocks[0], lines, per, 1)
    packed_all = packed_all.reshape(own, TAPS)
    highway_all[0] = highway_all[0].reshape(2 * own, FILTERS)

    def layer_bias(i):
        both = packed_all[:, taps_used + 1 + 2 * i : taps_used + 3 + 2 * i]
        return both.reshape(ndp, per, 2).transpose(0, 2, 1)[..., None]

    def both_sides(mine, theirs):
        mine = mine.reshape(ndp, 1, per, words)
        theirs = theirs.reshape(ndp, 1, per, words)
        first = jnp.where(side == 0, mine, theirs)
        second = jnp.where(side == 0, theirs, mine)
        return jnp.concatenate([first, second], axis=1).reshape(FILTERS, words)

    kept = []
    for i in range(layers):
        if i == 0:
            *highways, proj_all = gather_blocks(blocks[1:] + [proj_weight], lines, 2)
            highway_all[1:] = [h.reshape(2 * own, FILTERS) for h in highways]
            proj_all = proj_all.reshape(own, D)
        else:
            state_low = state.astype(bf16)
            other_low = pair_swap(state_low)
        state_full = both_sides(state_low, other_low)
        pre = dot(highway_all[i], state_full, 1, 0).reshape(ndp, 2, per, words) + layer_bias(i)
        nonlin = pre[:, 0].reshape(own, words)
        gate = jax.nn.sigmoid(pre[:, 1].reshape(own, words))
        kept.append((state, nonlin, gate, state_full, highway_all[i]))
        state = gate * state + (1.0 - gate) * gelu(nonlin)
    state_low = state.astype(bf16)
    emb_part = dot(state_low, proj_all, 0, 0)
    embedded = emb_part + pair_swap(emb_part.astype(bf16)).astype(f32) + proj_bias.astype(f32)

    emb_low = embedded.astype(bf16)
    seqs = words // LEN
    width = qkv_weight.shape[2]
    heads = width // HEAD_DIM
    qkv_t = qkv_weight.transpose(1, 0, 2)
    qkv_bias = jnp.stack([qv_bias[0], jnp.zeros_like(qv_bias[0]), qv_bias[1]]).astype(f32)
    projected = [
        (dot(emb_low, qkv_t[part], 1, 0) + qkv_bias[part][None]).astype(bf16) for part in range(3)
    ]

    def by_head(x):
        return x.reshape(-1, heads, HEAD_DIM).transpose(1, 0, 2)

    queries, keys, values = (by_head(part) for part in projected)
    scale = 1.0 / math.sqrt(HEAD_DIM)

    def probs_of(q):
        scores = jnp.einsum("hqd,hkd->hqk", q, keys, preferred_element_type=f32) * scale
        terms = jnp.exp(scores - jnp.max(scores, axis=-1, keepdims=True))
        return terms / jnp.sum(terms, axis=-1, keepdims=True)

    mixed = (
        jnp.einsum("hqk,hkd->qhd", probs_of(queries).astype(bf16), values, preferred_element_type=f32)
        .reshape(words, width)
        .astype(bf16)
    )
    att_part = dot(mixed, out_weight, 1, 0)
    gain_one, gain_two = ln1_gain.astype(f32), ln2_gain.astype(f32)
    summed = embedded + (
        att_part + pair_swap(att_part.astype(bf16)).astype(f32) + out_bias.astype(f32)
    )
    normalized_one, inv_std_one = norm_forward(summed)
    normed = normalized_one * gain_one + ln1_bias.astype(f32)
    normed_low = normed.astype(bf16)
    hidden = gelu(dot(normed_low, up_weight, 1, 0) + up_bias.astype(f32)).astype(bf16)
    ffn_part = dot(hidden, down_weight, 1, 0)

    slots = mask_pos.shape[1]
    padded_slots = -(-slots // 16) * 16
    positions = jnp.pad(mask_pos[0], (0, padded_slots - slots), constant_values=-1)
    pick = (positions[:, None] == jnp.arange(words, dtype=jnp.int32)[None, :]).astype(bf16)
    slot_grad = jnp.pad(out_grad[0], ((0, padded_slots - slots), (0, 0)))
    n1_high, n1_low = split_two(normalized_one)
    n1_s = dot(pick, n1_high, 1, 0) + dot(pick, n1_low, 1, 0)
    r1_s = jnp.sum(jnp.where(pick > 0, inv_std_one.T, 0.0), axis=1, keepdims=True)
    normed_s = n1_s * gain_one + ln1_bias.astype(f32)
    normed_low_s = dot(pick, normed_low, 1, 0).astype(bf16)
    mixed_s = dot(pick, mixed, 1, 0).astype(bf16)
    emb_s = dot(pick, emb_low, 1, 0).astype(bf16)
    queries_s = jnp.einsum("mw,hwd->hmd", pick, queries, preferred_element_type=f32).astype(bf16)
    hidden_pre_s = dot(normed_low_s, up_weight, 1, 0) + up_bias.astype(f32)
    hidden_s = gelu(hidden_pre_s).astype(bf16)
    ffn_s = dot(hidden_s, down_weight, 1, 0)

    theirs = lax.dynamic_slice_in_dim(ffn_part, (1 - side) * rows_here, rows_here, 0)
    got = pair_swap(jnp.concatenate([theirs, ffn_s], axis=0).astype(bf16)).astype(f32)
    start = side * rows_here
    second = (
        lax.dynamic_slice_in_dim(normed, start, rows_here, 0)
        + (lax.dynamic_slice_in_dim(ffn_part, start, rows_here, 0) + got[:rows_here])
        + down_bias.astype(f32)
    )
    normalized_two, _ = norm_forward(second)
    result = normalized_two * gain_two + ln2_bias.astype(f32)
    n2_s, r2_s = norm_forward(normed_s + (ffn_s + got[rows_here:]) + down_bias.astype(f32))

    grad_second = norm_backward(slot_grad, n2_s, r2_s, gain_two)
    ln2_gain_grad = jnp.sum(slot_grad * n2_s, axis=0)
    ln2_bias_grad = jnp.sum(slot_grad, axis=0)
    dffn = grad_second.astype(bf16)
    down_bias_grad = jnp.sum(dffn, axis=0, dtype=f32)
    down_grad_t = dot(dffn, hidden_s, 0, 0)
    dpre = (dot(dffn, down_weight, 1, 1) * gelu_both(hidden_pre_s)[1]).astype(bf16)
    up_bias_grad = jnp.sum(dpre, axis=0, dtype=f32)
    up_grad = dot(normed_low_s, dpre, 0, 0)
    dn_part = dot(dpre, up_weight, 1, 1)
    grad_normed = grad_second + (dn_part + pair_swap(dn_part.astype(bf16)).astype(f32))
    grad_first = norm_backward(grad_normed, n1_s, r1_s, gain_one)
    ln1_gain_grad = jnp.sum(grad_normed * n1_s, axis=0)
    ln1_bias_grad = jnp.sum(grad_normed, axis=0)
    dattn = grad_first.astype(bf16)
    out_bias_grad = jnp.sum(dattn, axis=0, dtype=f32)
    out_grad_t = dot(dattn, mixed_s, 0, 0)
    dmixed = by_head(dot(dattn, out_weight, 1, 1).astype(bf16))
    probs = probs_of(queries_s)
    dvalues = jnp.einsum("hqk,hqd->khd", probs.astype(bf16), dmixed, preferred_element_type=f32)
    dprobs = jnp.einsum("hqd,hkd->hqk", dmixed, values, preferred_element_type=f32)
    dscores = (probs * (dprobs - jnp.sum(probs * dprobs, axis=-1, keepdims=True))).astype(bf16)
    dqueries = jnp.einsum("hqk,hkd->qhd", dscores, keys, preferred_element_type=f32) * scale
    dkeys = jnp.einsum("hqk,hqd->khd", dscores, queries_s, preferred_element_type=f32) * scale
    dq = dqueries.reshape(padded_slots, width).astype(bf16)
    dk = dkeys.reshape(words, width).astype(bf16)
    dv = dvalues.reshape(words, width).astype(bf16)
    qv_bias_grad = jnp.stack([jnp.sum(dq, axis=0, dtype=f32), jnp.sum(dv, axis=0, dtype=f32)])
    qkvo_grad = [dot(emb_s, dq, 0, 0), dot(emb_low, dk, 0, 0), dot(emb_low, dv, 0, 0), out_grad_t]
    dq_high, dq_low = split_two(dot(dq, qkv_t[0], 1, 1))
    gf_high, gf_low = split_two(grad_first)
    back = dot(pick, jnp.concatenate([dq_high, gf_high], axis=1), 0, 0) + dot(
        pick, jnp.concatenate([dq_low, gf_low], axis=1), 0, 0
    )
    de_part = back[:, :D] + dot(dk, qkv_t[1], 1, 1) + dot(dv, qkv_t[2], 1, 1)
    encoder_grads = [
        g.astype(bf16).reshape(ndp, D // ndp, -1)
        for g in (up_grad, down_grad_t, jnp.concatenate(qkvo_grad, axis=1))
    ]
    first = side == 0
    shared = [
        jnp.where(first, g, 0.0)
        for g in (
            out_bias_grad, ln1_gain_grad, ln1_bias_grad, down_bias_grad, ln2_gain_grad, ln2_bias_grad,
        )
    ]
    own_side = jnp.concatenate([qv_bias_grad.reshape(-1), up_bias_grad])
    flat = jnp.concatenate([*shared, jnp.where(first, own_side, 0.0), jnp.where(first, 0.0, own_side)])
    rows_flat = -(-flat.shape[0] // 1024) * 8
    flat = jnp.pad(flat, (HEAD_ROWS * LANE, rows_flat * LANE - flat.shape[0])).reshape(-1, LANE)

    (up_mine, down_mine, qkvo_mine, proj_mine, *highway_mine, conv_mine), flat = embedder_backward(
        encoder_grads, de_part.astype(bf16), back[:, D:] + de_part, proj_all, state_low, packed_all,
        conv_all, lim, ids, flat, kept, pooled_raw, chars, lines, per, taps_used, 3,
    )
    highway_mine = highway_mine[::-1]
    table_grad_t = flat[:TABLE_ROWS].reshape(-1, CHAR_DIM, LANE).transpose(1, 0, 2).reshape(CHAR_DIM, -1)
    flat = flat[TABLE_ROWS:].reshape(-1)
    proj_bias_grad = flat[:D]
    flat = flat[(HEAD_ROWS - TABLE_ROWS) * LANE :]
    out_bias_grad, ln1_gain_grad, ln1_bias_grad, down_bias_grad, ln2_gain_grad, ln2_bias_grad = (
        flat[i * D : (i + 1) * D] for i in range(6)
    )
    at = 6 * D
    size = own_side.shape[0]
    own_side = jnp.where(first, flat[at : at + size], flat[at + size : at + 2 * size])
    qv_bias_grad = own_side[: 2 * width].reshape(2, width)
    up_bias_grad = own_side[2 * width :]
    conv_bias_mine = conv_mine[:, taps_used]
    highway_bias_mine = [
        conv_mine[:, taps_used + 1 + 2 * i : taps_used + 3 + 2 * i].T for i in range(layers)
    ]
    conv_mine = conv_mine[:, :taps_used]
    qkv_mine = jnp.stack([qkvo_mine[:, i * width : (i + 1) * width] for i in range(3)])
    out_mine = qkvo_mine[:, 3 * width :]
    highway_mine = jnp.stack(highway_mine).reshape(layers, 2, per, FILTERS).transpose(0, 3, 1, 2)
    highway_bias_mine = jnp.stack(highway_bias_mine).reshape(layers, 2, per)
    return (
        result.astype(bf16),
        table_grad_t.T[:ids_count],
        conv_mine.T,
        conv_bias_mine,
        highway_mine,
        highway_bias_mine,
        proj_mine,
        proj_bias_grad,
        qkv_mine.transpose(1, 0, 2),
        qv_bias_grad,
        out_mine.T,
        out_bias_grad,
        ln1_gain_grad,
        ln1_bias_grad,
        up_mine,
        up_bias_grad,
        down_mine.T,
        down_bias_grad,
        ln2_gain_grad,
        ln2_bias_grad,
    )


def solution(mesh):
    placed = (
        P(("dp", "tensor"), None),
        P("dp", None),
        P("dp", None, None),
        P(),
        P(None, ("dp", "tensor")),
        P(("dp", "tensor")),
        P(None, None, None, ("dp", "tensor")),
        P(None, None, ("dp", "tensor")),
        P(("dp", "tensor"), None),
        P(),
        P(None, None, "tensor"),
        P(None, "tensor"),
        P("tensor", None),
        P(),
        P(),
        P(),
        P(None, "tensor"),
        P("tensor"),
        P("tensor", None),
        P(),
        P(),
        P(),
    )
    return jax.shard_map(
        per_device,
        mesh=mesh,
        in_specs=placed,
        out_specs=(
            P(("dp", "tensor"), None),
            P(),
            P(None, ("dp", "tensor")),
            P(("dp", "tensor")),
            P(None, None, None, ("dp", "tensor")),
            P(None, None, ("dp", "tensor")),
            P(("dp", "tensor"), None),
            P(),
            P("dp", None, "tensor"),
            P(None, "tensor"),
            P("tensor", "dp"),
            P(),
            P(),
            P(),
            P("dp", "tensor"),
            P("tensor"),
            P("tensor", "dp"),
            P(),
            P(),
            P(),
        ),
        check_vma=False,
    )
```

```python
import functools
import math

import jax
import jax.numpy as jnp
from jax import lax
from jax.experimental import pallas as pl
from jax.experimental.pallas import tpu as pltpu
from jax.sharding import PartitionSpec as P

HEAD_DIM = 64
FILTERS = 2048
CHAR_DIM = 16
CHARS = 50
MAX_WIDTH = 7
LEN = 512
D = 768

channel_shares = (1, 2, 4, 8, 16, 32)
norm_eps = 1e-05
big_negative = -1e30
f32 = jnp.float32
bf16 = jnp.bfloat16
PAIR = "tensor"
GROUP = "dp"
TAPS = 128
VROWS = (CHARS + 7) * CHAR_DIM
FBLOCK = 256


def gelu(x):
    return 0.5 * x * (1.0 + lax.erf(x * (1.0 / math.sqrt(2.0))))


def gelu_both(x):
    share = 0.5 * (1.0 + lax.erf(x * (1.0 / math.sqrt(2.0))))
    return x * share, share + x * jnp.exp(-0.5 * x * x) * (1.0 / math.sqrt(2.0 * math.pi))


def width_of(channel):
    return 1 + sum(channel >= part * (FILTERS // 64) for part in channel_shares)


def dot(a, b, ca, cb):
    return lax.dot_general(a, b, (((ca,), (cb,)), ((), ())), preferred_element_type=f32)


def block_limits(per, start, stop):
    widths = [
        width_of((row // per) * 2 * per + side * per + row % per)
        for row in range(start, stop)
        for side in range(2)
    ]
    return CHARS + 1 - max(widths), CHARS + 1 - min(widths)


MESH = pl.DeviceIdType.MESH
ANYWHERE = pl.BlockSpec(memory_space=pl.ANY)


def pair_swap(x):
    return lax.ppermute(x, PAIR, [(0, 1), (1, 0)])


class Place:
    def __init__(self, lines):
        self.lines = lines
        index = lax.axis_index(GROUP)
        self.side = lax.axis_index(PAIR)
        self.line, self.row, self.core = index // 4, (index // 2) % 2, index % 2
        self.sibling = self.at(self.line, self.row, 1 - self.core)
        self.across = self.at(self.line, 1 - self.row, self.core)
        self.partner = (index, 1 - self.side)
        self.depth = (lines - 1).bit_length()
        self.bits = {"y": self.row}
        for i in range(self.depth):
            self.bits[f"z{i}"] = (self.line // 2**i) % 2

    def at(self, line, row, core):
        return ((line * 2 + row) * 2 + core, self.side)

    def flip(self, name):
        if name == "y":
            return self.across
        span = 2 ** int(name[1:])
        return self.on_line(self.line + span - 2 * span * self.bits[name])

    def on_line(self, line):
        return self.at(line, self.row, self.core)


def send(source, target, sems, device):
    copy = pltpu.make_async_remote_copy(
        src_ref=source, dst_ref=target, send_sem=sems[0], recv_sem=sems[1],
        device_id=device, device_id_type=MESH,
    )
    copy.start()
    return copy


def meet(devices):
    barrier = pltpu.get_barrier_semaphore()
    for device in devices:
        pl.semaphore_signal(barrier, inc=1, device_id=device, device_id_type=MESH)
    pl.semaphore_wait(barrier, len(devices))


class Gather:
    def __init__(self, place, blocks, wholes, sems):
        self.place, self.blocks, self.wholes = place, blocks, wholes
        self.line_s, self.line_r, self.row_s, self.row_r, self.core_s, self.core_r, self.own = sems

    def piece(self, k, line, row, core):
        return self.wholes[k].at[line, row, core]

    def to_line(self, k, source, line, step):
        p = self.place
        return pltpu.make_async_remote_copy(
            src_ref=source, dst_ref=self.piece(k, line, p.row, p.core),
            send_sem=self.line_s.at[k, line, 0 if step > 0 else 1], recv_sem=self.line_r.at[k, line],
            device_id=p.on_line(lax.rem(p.line + step + p.lines, p.lines)), device_id_type=MESH,
        )

    def to_row(self, k, source, line):
        p = self.place
        return pltpu.make_async_remote_copy(
            src_ref=source, dst_ref=self.piece(k, line, p.row, p.core),
            send_sem=self.row_s.at[k, line], recv_sem=self.row_r.at[k, line],
            device_id=p.across, device_id_type=MESH,
        )

    def to_core(self, k, source, line, row):
        p = self.place
        return pltpu.make_async_remote_copy(
            src_ref=source, dst_ref=self.piece(k, line, row, p.core),
            send_sem=self.core_s.at[k, line, row], recv_sem=self.core_r.at[k, line, row],
            device_id=p.sibling, device_id_type=MESH,
        )

    def pass_on(self, k, line, source, left, right):
        p = self.place
        if right:
            @pl.when(p.line < p.lines - 1)
            def _():
                self.to_line(k, source, line, 1).start()
        if left:
            @pl.when(p.line > 0)
            def _():
                self.to_line(k, source, line, -1).start()
        self.to_row(k, source, line).start()
        self.to_core(k, source, line, p.row).start()

    def begin(self, k):
        p = self.place
        pltpu.make_async_copy(self.blocks[k], self.piece(k, p.line, p.row, p.core), self.own.at[k]).start()
        self.pass_on(k, p.line, self.blocks[k], True, True)

    def from_row(self, k, line):
        p = self.place
        got = self.piece(k, line, 1 - p.row, p.core)
        pltpu.make_async_remote_copy(
            src_ref=got, dst_ref=got, send_sem=self.row_s.at[k, line], recv_sem=self.row_r.at[k, line],
            device_id=p.across, device_id_type=MESH,
        ).wait_recv()
        self.to_core(k, got, line, 1 - p.row).start()

    def turn(self, k, r):
        p = self.place
        for step in (1, -1):
            line = p.line - step * r
            inside = (line >= 0) & (line < p.lines)

            @pl.when(inside)
            def _(line=line, step=step):
                got = self.piece(k, line, p.row, p.core)
                self.to_line(k, got, line, step).wait_recv()
                self.pass_on(k, line, got, step < 0, step > 0)
        self.crossed(k, r - 1)

    def crossed(self, k, r):
        p = self.place
        for step in (1, -1) if r else (1,):
            line = p.line - step * r
            inside = (line >= 0) & (line < p.lines)

            @pl.when(inside)
            def _(line=line):
                self.from_row(k, line)

    def finish(self, k):
        p = self.place
        self.crossed(k, p.lines - 1)
        own = self.piece(k, p.line, p.row, p.core)
        pltpu.make_async_copy(self.blocks[k], own, self.own.at[k]).wait()

        def each(line, carry):
            for row in range(2):
                self.to_core(k, self.piece(k, line, row, p.core), line, row).wait_send()
                self.to_core(k, self.piece(k, line, row, 1 - p.core), line, row).wait_recv()
            self.to_row(k, self.piece(k, line, p.row, p.core), line).wait_send()

            @pl.when((p.line < p.lines - 1) & (line <= p.line))
            def _():
                self.to_line(k, self.piece(k, line, p.row, p.core), line, 1).wait_send()

            @pl.when((p.line > 0) & (line >= p.line))
            def _():
                self.to_line(k, self.piece(k, line, p.row, p.core), line, -1).wait_send()
            return carry

        lax.fori_loop(0, p.lines, each, 0)

    @staticmethod
    def sems(count, lines):
        dma = pltpu.SemaphoreType.DMA
        return [
            dma((count, lines, 2)), dma((count, lines)), dma((count, lines)), dma((count, lines)),
            dma((count, lines, 2)), dma((count, lines, 2)), dma((count,)),
        ]


def neighbours(place, partner):
    others = [
        place.on_line(lax.rem(place.line + step, place.lines)) for step in range(1, place.lines)
    ]
    return [place.sibling, place.across, *others] + ([place.partner] if partner else [])


class Scatter:
    def __init__(self, place, arrays, land, outs, pieces, orders, bufs, sems):
        self.place, self.arrays, self.land, self.outs = place, arrays, land, outs
        self.pieces, self.orders = pieces, orders
        self.stages = place.depth + 2
        self.parts, self.got = bufs[: self.stages - 1], bufs[self.stages - 1 :]
        self.send_s, self.recv_s, self.load = sems
        self.begun, self.loads = set(), {}

    def span(self, k):
        array, start, size = self.pieces[k]
        return array, pl.ds(start, size), size, self.arrays[array].shape[-1]

    def axes(self, k, stage):
        left = [f"z{i}" for i in reversed(range(self.place.depth))] + ["y"]
        for name in self.orders[k][: stage - 1]:
            left.remove(name)
        return len(left), left.index(self.orders[k][stage - 1])

    def slot(self, k, stage):
        return k % self.parts[stage].shape[0]

    def copy(self, k, stage):
        array, rows, size, width = self.span(k)
        p = self.place
        if stage == 0:
            source = self.arrays[array].at[(slice(None),) * (p.depth + 1) + (1 - p.core, rows)]
            device = p.sibling
            count = p.depth + 1
        else:
            count, axis = self.axes(k, stage)
            name = self.orders[k][stage - 1]
            index = [slice(None)] * count
            index[axis] = 1 - p.bits[name]
            source = self.parts[stage - 1].at[
                (self.slot(k, stage - 1), *index, pl.ds(0, size), pl.ds(0, width))
            ]
            device = p.flip(name)
            count -= 1
        return pltpu.make_async_remote_copy(
            src_ref=source, dst_ref=self.land[stage][array].at[(slice(None),) * count + (rows,)],
            send_sem=self.send_s.at[k, stage], recv_sem=self.recv_s.at[k, stage],
            device_id=device, device_id_type=MESH,
        )

    def begin(self, k):
        self.copy(k, 0).start()
        self.begun.add(k)

    def fetch(self, k, stage):
        array, rows, size, width = self.span(k)
        count = self.stages - 1 - stage
        every = (slice(None),) * count
        here = every + (pl.ds(0, size), pl.ds(0, width))
        copies = []
        if stage == 0:
            if k >= self.parts[0].shape[0]:
                self.copy(k - self.parts[0].shape[0], 1).wait_send()
            own = self.arrays[array].at[every + (self.place.core, rows)]
            there = self.parts[0].at[(self.slot(k, 0), *here)]
            copies.append(pltpu.make_async_copy(own, there, self.load.at[self.stages]))
            copies[0].start()
        self.copy(k, stage).wait_recv()
        copies.append(
            pltpu.make_async_copy(
                self.land[stage][array].at[every + (rows,)], self.got[stage].at[here], self.load.at[stage]
            )
        )
        copies[-1].start()
        self.loads[k, stage] = copies

    def add(self, k, stage):
        array, rows, size, width = self.span(k)
        p = self.place
        final = stage == self.stages - 1
        if (k, stage) not in self.loads:
            self.fetch(k, stage)
        if not final and stage and k >= self.parts[stage].shape[0]:
            self.copy(k - self.parts[stage].shape[0], stage + 1).wait_send()
        for copy in self.loads.pop((k, stage)):
            copy.wait()
        count = self.stages - 1 - stage
        if stage:
            _, axis = self.axes(k, stage)
            bit = p.bits[self.orders[k][stage - 1]]

        def each(i, carry):
            part = pl.ds(pl.multiple_of((i % (size // 16)) * 16, 16), 16)
            which = i // (size // 16)
            index = [(which // 2 ** (count - 1 - j)) % 2 for j in range(count)]
            there = self.got[stage][(*index, part, slice(0, width))]
            if stage == 0:
                here = self.parts[0][(self.slot(k, 0), *index, part, slice(0, width))]
            else:
                inner = index[:axis] + [bit] + index[axis:]
                here = self.parts[stage - 1][
                    (self.slot(k, stage - 1), *inner, part, slice(0, width))
                ]
            if final:
                at = pl.ds(pl.multiple_of(self.pieces[k][1] + i * 16, 16), 16)
                self.outs[array][at, :] = here.astype(f32) + there.astype(f32)
            else:
                self.parts[stage][(self.slot(k, stage), *index, part, slice(0, width))] = here + there
            return carry

        lax.fori_loop(0, 2**count * (size // 16), each, 0)
        if not final:
            self.copy(k, stage + 1).start()
        if stage == 0 and k + 1 in self.begun:
            self.fetch(k + 1, 0)

    def order(self, count):
        work = []
        lead = self.parts[0].shape[0] - 1
        last = self.stages - 1
        for k in range(count + lead + 2 * last):
            steps = [(k - lead - 2 * (s - 1), s) for s in range(last, 0, -1)]
            work += [(self.add, j, s) for j, s in steps if 0 <= j < count]
            if k < count:
                work.append((self.add, k, 0))
            work += [(self.fetch, j + 1, s) for j, s in steps if 0 <= j + 1 < count]
        return work
        return work

    def finish(self):
        count = len(self.pieces)
        for k in range(count):
            self.copy(k, 0).wait_send()
            for stage in range(1, self.stages):
                if k >= count - self.parts[stage - 1].shape[0]:
                    self.copy(k, stage).wait_send()

    @staticmethod
    def shapes(arrays, pieces, depth):
        lead = lambda stage: (2,) * (depth + 1 - stage)
        land = [
            jax.ShapeDtypeStruct(lead(stage) + a.shape[-2:], bf16)
            for stage in range(depth + 2)
            for a in arrays
        ]
        outs = [jax.ShapeDtypeStruct(a.shape[-2:], f32) for a in arrays]
        tile = (max(size for _, _, size in pieces), max(a.shape[-1] for a in arrays))
        dma = pltpu.SemaphoreType.DMA
        count = len(pieces)
        slots = 4 if depth <= 3 else 2
        bufs = [pltpu.VMEM((slots,) + lead(0) + tile, bf16)]
        bufs += [pltpu.VMEM((2,) + lead(stage) + tile, bf16) for stage in range(1, depth + 1)]
        bufs += [pltpu.VMEM(lead(stage) + tile, bf16) for stage in range(depth + 2)]
        sems = [dma((count, depth + 2)), dma((count, depth + 2)), dma((depth + 3,))]
        return land, outs, bufs, sems


def cut(arrays, most):
    pieces = []
    for i, a in enumerate(arrays):
        rows = a.shape[-2]
        size = max(s for s in range(16, most + 1, 16) if rows % s == 0)
        pieces += [(i, start, size) for start in range(0, rows, size)]
    return pieces


def onehot_chars(ids_row, count):
    return jnp.where(
        lax.broadcasted_iota(jnp.int32, (count, ids_row.shape[1]), 0) == ids_row, 1.0, 0.0
    ).astype(bf16)


class Pooling:
    group = 32

    def __init__(self, limits, chars, weight, lim, pooled, bufs):
        self.limits, self.chars, self.weight, self.lim = limits, chars, weight, lim
        self.pooled, self.bufs = pooled, bufs
        self.halves = chars.shape[1] // FBLOCK
        self.units = [(b, h) for b in range(len(limits)) for h in range(self.halves)]

    def convolve(self, u, p):
        block, half = self.units[u]
        rows = pl.ds(pl.multiple_of(p * CHAR_DIM, CHAR_DIM), TAPS)
        taps = self.chars[rows, pl.ds(half * FBLOCK, FBLOCK)]
        self.bufs[u % 2][p] = dot(self.weight[pl.ds(block * FBLOCK, FBLOCK), :], taps, 1, 0)

    def pool(self, u, g):
        block, half = self.units[u]
        full, some = self.limits[block]
        buf, size = self.bufs[u % 2], self.group
        here = pl.ds(pl.multiple_of(g * size, size), size)
        there = pl.ds(pl.multiple_of(block * FBLOCK + g * size, size), size)
        lim = self.lim[there, :] if some > full else None

        def entry(p):
            value = buf[p, here, :]
            return value if p < full else jnp.where(lim[:, :1] >= p, value, big_negative)

        top = entry(0)
        for p in range(1, some):
            top = jnp.maximum(top, entry(p))
        total = jnp.exp(entry(0) - top)
        for p in range(1, some):
            total = total + jnp.exp(entry(p) - top)
        self.pooled[there, pl.ds(half * FBLOCK, FBLOCK)] = top + jnp.log(total)

    def step(self, u):
        count = FBLOCK // self.group
        todo = self.limits[self.units[u][0]][1] if u < len(self.units) else 0
        each = -(-todo // count)

        def body(g, carry):
            for i in range(each):
                self.convolve(u, jnp.minimum(g * each + i, todo - 1))
            if u:
                self.pool(u - 1, g)
            return carry

        lax.fori_loop(0, count, body, 0)


def forward_kernel(
    lines, limits, per, taps_used, ids_ref, table_ref, lim_ref, packed_ref, first_ref, second_ref, proj_ref,
    bias_ref,
    packed_all, first_all, second_all, proj_all, both_a, nonlin_a, gate_a, ids_all, chars_ref, weight_ref,
    pooled_ref, state_ref, state_b, both_b, nonlin_b, gate_b, low_ref, emb_ref,
    buf_a, buf_b, packed_vmem, bias_all, low_b, other_ref, come, wbuf, pre, proj, leave, arrive, ids_s, ids_r, load,
    state_s, state_r, weight_s, proj_s, keep_s, swap_s, swap_r, emb_s, emb_r, *sems,
):
    place = Place(lines)
    half = first_ref.shape[0] // 2
    wide = [(ref, whole) for ref, whole in ((first_ref, first_all), (second_ref, second_all))]
    gather = Gather(
        place,
        [packed_ref]
        + [ref.at[pl.ds(i * half, half)] for ref, _ in wide for i in range(2)]
        + [proj_ref],
        [packed_all]
        + [whole.at[:, :, :, pl.ds(i * half, half)] for _, whole in wide for i in range(2)]
        + [proj_all],
        sems,
    )
    near, far = (1, 2), (3, 4, 5)
    meet(neighbours(place, True))
    gather.begin(0)
    ids_copy = send(ids_ref, ids_all.at[place.side], (ids_s, ids_r), place.partner)
    own_copy = pltpu.make_async_copy(ids_ref, ids_all.at[place.side], load)
    own_copy.start()
    for k in near:
        gather.begin(k)
    own_copy.wait()
    ids_copy.wait()
    count = ids_ref.shape[0]

    def embed(c, carry):
        for i in range(5):
            row = pl.ds(c * 5 + i, 1)
            ids = jnp.concatenate([ids_all[0, row, :], ids_all[1, row, :]], axis=1)
            hot = onehot_chars(ids, table_ref.shape[1])
            rows = pl.ds(pl.multiple_of((c * 5 + i) * CHAR_DIM, CHAR_DIM), CHAR_DIM)
            chars_ref[rows, :] = dot(table_ref[...], hot, 1, 0).astype(bf16)
        return carry

    lax.fori_loop(0, count // 5, embed, 0)
    words = chars_ref.shape[1]
    chars_ref[CHARS * CHAR_DIM :, :] = jnp.zeros((VROWS - CHARS * CHAR_DIM, words), bf16)
    for r in range(1, lines):
        gather.turn(0, r)
    gather.finish(0)
    copy = pltpu.make_async_copy(packed_all, packed_vmem, load)
    copy.start()
    copy.wait()
    rows = weight_ref.shape[0]
    packed = packed_vmem[...].reshape(rows, TAPS)
    shift = lax.broadcasted_iota(jnp.int32, (rows, TAPS), 1)
    keep = (shift < (CHARS - lim_ref[...]) * CHAR_DIM) & (shift < MAX_WIDTH * CHAR_DIM)
    weight_ref[...] = jnp.where(keep, packed, 0.0).astype(bf16)
    bias_all[...] = packed
    for k in near:
        gather.turn(k, 1)
    own, words = pooled_ref.shape
    quarter = own // 4
    lines_each = lines // 4

    def packed_lane(rows, lane):
        return bias_all[rows, lane : lane + 1]

    pooling = Pooling(limits, chars_ref, weight_ref, lim_ref, pooled_ref, (buf_a, buf_b))
    steps = len(pooling.units) + 1
    state_copies = []
    later = {2: (near, 2), 5: (near, 3), 6: (far, 0), 8: (far, 1)} if lines == 4 else {}
    for u in range(steps):
        pooling.step(u)
        done = u - 1
        if done >= 0 and done % pooling.halves == pooling.halves - 1:
            block = done // pooling.halves
            span = pl.ds(block * FBLOCK, FBLOCK)
            state = gelu(pooled_ref[span, :] + packed_lane(span, taps_used))
            state_ref[span, :] = state
            low_ref[span, :] = state.astype(bf16)
            state_copies.append(
                send(
                    low_ref.at[span], other_ref.at[span], (state_s.at[block], state_r.at[block]),
                    place.partner,
                )
            )
        if u in later:
            for k in later[u][0]:
                if later[u][1]:
                    gather.turn(k, later[u][1])
                else:
                    gather.begin(k)
    if not later:
        for r in range(2, lines):
            for k in near:
                gather.turn(k, r)
        for k in far:
            gather.begin(k)
        for k in far:
            gather.turn(k, 1)
    for k in near:
        gather.finish(k)
    for copy in state_copies:
        copy.wait()

    def weights(source, q):
        copy = pltpu.make_async_copy(
            source.at[pl.ds(q * lines_each, lines_each)], wbuf.at[q % 2], weight_s.at[q % 2]
        )
        copy.start()
        return copy

    def assemble(mine_ref, theirs_ref):
        def each(c, carry):
            rows = pl.ds(pl.multiple_of(c * 64, 64), 64)
            mine, theirs = mine_ref[rows, :], theirs_ref[rows, :].astype(f32)
            first = jnp.where(place.side == 0, mine, theirs).reshape(64 // per, per, words)
            second = jnp.where(place.side == 0, theirs, mine).reshape(64 // per, per, words)
            both = jnp.stack([first, second], axis=1).reshape(128, words)
            both_b[pl.ds(pl.multiple_of(c * 128, 128), 128), :] = both.astype(bf16)
            return carry

        lax.fori_loop(0, own // 64, each, 0)

    def layer(l, source, before, after, low_out, copies, done):
        for q in range(4):
            copies[q % 2].wait()

            def product(n, carry, q=q):
                lanes = pl.ds(pl.multiple_of(n * 256, 256), 256)
                pre[:, lanes] = dot(wbuf[q % 2].reshape(2 * quarter, FILTERS), both_b[:, lanes], 1, 0)
                return carry

            lax.fori_loop(0, words // 256, product, 0)
            if q < 2:
                copies[q % 2] = weights(source, q + 2)

            def activate(c, carry, q=q):
                rows = pl.ds(pl.multiple_of(q * quarter + c * 64, 64), 64)
                part = pre[pl.ds(pl.multiple_of(c * 128, 128), 128), :].reshape(64 // per, 2, per, words)
                at = taps_used + 1 + 2 * l
                nonlin = part[:, 0].reshape(64, words) + packed_lane(rows, at)
                gate = jax.nn.sigmoid(part[:, 1].reshape(64, words) + packed_lane(rows, at + 1))
                value = gate * before[rows, :] + (1.0 - gate) * gelu(nonlin)
                nonlin_b[rows, :] = nonlin
                gate_b[rows, :] = gate
                if after is not None:
                    after[rows, :] = value
                low_out[rows, :] = value.astype(bf16)
                return carry

            lax.fori_loop(0, quarter // 64, activate, 0)
            done(q)

    swaps = []

    def swap(q):
        rows = pl.ds(q * quarter, quarter)
        swaps.append(send(low_b.at[rows], come.at[rows], (swap_s.at[q], swap_r.at[q]), place.partner))
        if q == 1 and lines > 3:
            for k in far:
                gather.turn(k, 2)

    copies = [weights(first_all, 0), weights(first_all, 1)]
    assemble(state_ref, other_ref)
    layer(0, first_all, state_ref, state_b, low_b, copies, swap)
    kept = [
        pltpu.make_async_copy(source, target, keep_s.at[i])
        for i, (source, target) in enumerate(((both_b, both_a), (nonlin_b, nonlin_a), (gate_b, gate_a)))
    ]
    for copy in kept:
        copy.start()
    for r in range(3, lines):
        for k in far:
            gather.turn(k, r)
    for copy in swaps:
        copy.wait()
    for copy in kept:
        copy.wait()
    assemble(state_b, come)
    for k in far:
        gather.finish(k)
    copies = [weights(second_all, 0), weights(second_all, 1)]
    proj_copy = pltpu.make_async_copy(proj_all, proj, proj_s)
    proj_copy.start()
    layer(1, second_all, state_b, None, low_ref, copies, lambda q: None)
    proj_copy.wait()

    sends = []
    for c in range(words // LANE):
        rows = pl.ds(c * LANE, LANE)
        part = dot(low_ref[:, c * LANE : (c + 1) * LANE], proj[...].reshape(own, D), 0, 0)
        emb_ref[rows, :] = part + bias_ref[...]
        leave[rows, :] = part.astype(bf16)
        sends.append(
            send(leave.at[rows], arrive.at[rows], (emb_s.at[c], emb_r.at[c]), place.partner)
        )
    for c, copy in enumerate(sends):
        rows = pl.ds(c * LANE, LANE)
        copy.wait()
        emb_ref[rows, :] = emb_ref[rows, :] + arrive[rows, :].astype(f32)


def embedder_forward(
    ids, table, lim, packed, first, second, proj, bias, lines, per, taps_used, ident
):
    own = lim.shape[0]
    words = 2 * ids.shape[1]
    limits = tuple(block_limits(per, s, s + FBLOCK) for s in range(0, own, FBLOCK))
    lead = (lines, 2, 2)
    shape = jax.ShapeDtypeStruct
    vmem = pl.BlockSpec(memory_space=pltpu.VMEM)
    dma = pltpu.SemaphoreType.DMA
    full = shape((own, words), f32)
    both = shape((2 * own, words), bf16)
    blocks = len(limits)
    return pl.pallas_call(
        functools.partial(forward_kernel, lines, limits, per, taps_used),
        out_shape=(
            shape(lead + packed.shape, f32), shape(lead + first.shape, bf16),
            shape(lead + second.shape, bf16), shape(lead + proj.shape, bf16), both, full, full,
            shape((2,) + ids.shape, jnp.int32), shape((VROWS, words), bf16), shape((own, TAPS), bf16),
            full, full, full, both, full, full, shape((own, words), bf16), shape((words, D), f32),
        ),
        in_specs=[vmem, vmem, vmem, ANYWHERE, ANYWHERE, ANYWHERE, ANYWHERE, vmem],
        out_specs=tuple([ANYWHERE] * 7 + [vmem] * 11),
        scratch_shapes=[
            pltpu.VMEM((CHARS, FBLOCK, FBLOCK), f32), pltpu.VMEM((CHARS, FBLOCK, FBLOCK), f32),
            pltpu.VMEM(lead + packed.shape, f32), pltpu.VMEM((own, TAPS), f32),
            pltpu.VMEM((own, words), bf16), pltpu.VMEM((own, words), bf16), pltpu.VMEM((own, words), bf16),
            pltpu.VMEM((2, lines // 4, 2, 2, 2 * per, FILTERS), bf16),
            pltpu.VMEM((own // 2, words), f32),
            pltpu.VMEM(lead + proj.shape, bf16),
            pltpu.VMEM((words, D), bf16), pltpu.VMEM((words, D), bf16),
            dma, dma, dma, dma((blocks,)), dma((blocks,)), dma((2,)), dma, dma((3,)), dma((4,)), dma((4,)),
            dma((words // LANE,)), dma((words // LANE,)), *Gather.sems(6, lines),
        ],
        compiler_params=pltpu.CompilerParams(
            collective_id=ident, has_side_effects=True, vmem_limit_bytes=62 << 20
        ),
    )(ids, table, lim, packed, first, second, proj, bias)


LANE = 128
TABLE_ROWS = 48
HEAD_ROWS = 56


class Totals:
    def __init__(self, place, value, inbox, send_sems, recv_sems):
        self.place, self.value, self.inbox = place, value, inbox
        self.send_sems, self.recv_sems = send_sems, recv_sems
        self.partners = [place.sibling, place.across]
        self.partners += [place.flip(f"z{i}") for i in range(place.depth)] + [place.partner]

    def start(self, i):
        self.copy = send(
            self.value, self.inbox.at[i], (self.send_sems.at[i], self.recv_sems.at[i]), self.partners[i]
        )

    def end(self, i):
        self.copy.wait()
        self.value[...] = self.value[...] + self.inbox[i]


def bias_lane(rows, lane, value):
    return jnp.where(lax.broadcasted_iota(jnp.int32, (rows, LANE), 1) == lane, value, 0.0)


def back_kernel(lines, limits, per, pieces, orders, taps_used, *refs):
    refs = iter(refs)

    def take(n):
        return [next(refs) for _ in range(n)]

    enc = take(3)
    (de_ref, base_ref, proj_ref, low_ref, packed_ref, conv_ref, conv_t_ref, lim_ref, ids_ref, vec_in) = take(10)
    kept_hbm = [take(5), take(5)]
    pooled_hbm, chars_hbm = take(2)
    depth = (lines - 1).bit_length()
    land = [take(7) for _ in range(depth + 2)]
    highway_hbm = take(2)
    outs = take(6)
    outs[4:5] = [outs[4].at[1], outs[4].at[0]]
    (vec_ref,) = take(1)
    scatter_bufs, scatter_sems = take(2 * depth + 3), take(3)
    (kst, knl, kgt, full, wbuf, acc, dpre, dpre_t, gs) = take(9)
    (demb, leave, come, projg, convg, pack, chars, inbox) = take(8)
    (load_s, weight_s, out_s, swap_s, swap_r, total_s, total_r) = take(7)

    place = Place(lines)
    side = place.side
    arrays = [*enc, projg, highway_hbm[1], highway_hbm[0], convg]
    scatter = Scatter(place, arrays, land, outs, pieces, orders, scatter_bufs, scatter_sems)
    of_array = [[k for k, piece in enumerate(pieces) if piece[0] == i] for i in range(7)]
    main = of_array[6][0]
    ticks = scatter.order(main)
    meet(neighbours(place, True))

    def go(k, stage):
        while (scatter.add, k, stage) in ticks:
            call, *which = ticks.pop(0)
            call(*which)

    def begin(i):
        for k in of_array[i]:
            scatter.begin(k)

    own, words = gs.shape
    quarter = own // 4
    inner = (slice(None),) * (depth - 2 + 3)

    def bits_of(index):
        return tuple((index // 2**i) % 2 for i in reversed(range(depth + 2)))


    def loads(layer):
        state, nonlin, gate, both, _ = kept_hbm[layer]
        copies = [
            pltpu.make_async_copy(src, dst, load_s.at[i])
            for i, (src, dst) in enumerate(((state, kst), (nonlin, knl), (gate, kgt), (both, full)))
        ]
        for copy in copies:
            copy.start()
        return copies

    def weights(layer, q):
        copy = pltpu.make_async_copy(
            kept_hbm[layer][4].at[q // 2, q % 2], wbuf.at[q % 2], weight_s.at[q % 2]
        )
        copy.start()
        return copy

    kept_copies = loads(1)
    weight_copies = [weights(1, 0), weights(1, 1)]
    de_copy = send(de_ref, demb, (swap_s.at[2, 0], swap_r.at[2, 0]), place.partner)
    for i in range(3):
        begin(i)
    vec_ref[...] = vec_in[...]
    pack[...] = jnp.zeros_like(pack)
    go(2, 0)
    de_copy.wait()

    total = jnp.zeros((1, demb.shape[1]), f32)
    for c in range(words // LANE):
        rows = pl.ds(c * LANE, LANE)
        value = (base_ref[rows, :] + demb[rows, :].astype(f32)).astype(bf16)
        demb[rows, :] = value
        total = total + jnp.sum(value.astype(f32), axis=0, keepdims=True)
    total = jnp.where(side == 0, total, 0.0)
    for j in range(demb.shape[1] // LANE):
        vec_ref[TABLE_ROWS + j : TABLE_ROWS + j + 1, :] = total[:, j * LANE : (j + 1) * LANE]

    def project(c, carry):
        rows = pl.ds(pl.multiple_of(c * LANE, LANE), LANE)
        grad = dot(low_ref[rows, :], demb[...], 1, 0)
        for j in range(LANE // per):
            index = bits_of(c * (LANE // per) + j)
            projg[(*index, slice(0, per))] = grad[j * per : (j + 1) * per].astype(bf16)
        gs[rows, :] = dot(proj_ref[rows, :], demb[...], 1, 1)
        return carry

    lax.fori_loop(0, own // LANE, project, 0)
    begin(3)
    go(0, 1)

    def quarter_rows(c, q):
        return pl.ds(pl.multiple_of(q * quarter + c * 64, 64), 64)

    def arrive(l, q):
        swaps[l, q].wait()

        def add(c, carry):
            rows = quarter_rows(c, q)
            gs[rows, :] += come[l, rows, :].astype(f32)
            return carry

        lax.fori_loop(0, quarter // 64, add, 0)

    def layer(l, marks):
        for copy in kept_copies:
            copy.wait()
        for q in range(4):
            if l + 1 < 2:
                arrive(l + 1, q)

            def slopes(c, carry, q=q):
                rows = quarter_rows(c, q)
                grad, nonlin, gate = gs[rows, :], knl[rows, :], kgt[rows, :]
                through = grad * (1.0 - gate)
                value, slope = gelu_both(nonlin)
                d_nonlin = through * slope
                d_gate = grad * (kst[rows, :] - value) * gate * (1.0 - gate)
                gs[rows, :] = grad * gate
                both = jnp.stack(
                    [d_nonlin.reshape(64 // per, per, words), d_gate.reshape(64 // per, per, words)], axis=1
                ).reshape(128, words)
                there = pl.ds(pl.multiple_of(2 * quarter * q + c * 128, 128), 128)
                dpre[there, :] = both.astype(bf16)
                dpre_t[:, there] = both.T.astype(bf16)
                at = taps_used + 1 + 2 * l
                pack[rows, :] += bias_lane(64, at, jnp.sum(d_nonlin, axis=1, keepdims=True)) + bias_lane(
                    64, at + 1, jnp.sum(d_gate, axis=1, keepdims=True)
                )
                return carry

            lax.fori_loop(0, quarter // 64, slopes, 0)
            weight_copies[q % 2].wait()

            def back(n, carry, q=q):
                lanes = pl.ds(pl.multiple_of(n * 256, 256), 256)
                matrix = wbuf[(q % 2, *inner, lanes)].reshape(2 * quarter, 256)
                part = dot(dpre_t[:, 2 * quarter * q : 2 * quarter * (q + 1)], matrix, 1, 0)
                if q:
                    part = acc[:, lanes] + part
                acc[:, lanes] = part
                return carry

            lax.fori_loop(0, FILTERS // 256, back, 0)
            if q < 2:
                weight_copies[q % 2] = weights(l, q + 2)
            if marks[q]:
                go(*marks[q])
        for q in range(4):
            def turn(c, carry, q=q):
                lanes = pl.ds(pl.multiple_of(2 * quarter * q + c * 128, 128), 128)
                part = acc[:, lanes].T.reshape(64 // per, 2, per, words)
                first, second = part[:, 0].reshape(64, words), part[:, 1].reshape(64, words)
                rows = quarter_rows(c, q)
                gs[rows, :] += jnp.where(side == 0, first, second)
                leave[rows, :] = jnp.where(side == 0, second, first).astype(bf16)
                return carry

            lax.fori_loop(0, quarter // 64, turn, 0)
            rows = pl.ds(q * quarter, quarter)
            swaps[l, q] = send(
                leave.at[rows], come.at[l, rows], (swap_s.at[l, q], swap_r.at[l, q]), place.partner
            )
        stores = [None, None]
        for q in range(4):
            if stores[q % 2] is not None:
                stores[q % 2].wait()

            def grads(n, carry, q=q):
                lanes = pl.ds(pl.multiple_of(n * 256, 256), 256)
                part = dot(dpre[2 * quarter * q : 2 * quarter * (q + 1), :], full[lanes, :], 1, 1)
                wbuf[(q % 2, *inner, lanes)] = part.astype(bf16).reshape(wbuf.shape[1:-1] + (256,))
                return carry

            lax.fori_loop(0, FILTERS // 256, grads, 0)
            stores[q % 2] = pltpu.make_async_copy(
                wbuf.at[q % 2], highway_hbm[l].at[q // 2, q % 2], out_s.at[q % 2]
            )
            stores[q % 2].start()
        for store in stores:
            store.wait()

    swaps = {}
    first_hw = [of_array[4][0], of_array[5][0]]
    layer(1, [None, (first_hw[0] - 1, 0), None, (1, 1)])
    kept_copies = loads(0)
    weight_copies = [weights(0, 0), weights(0, 1)]
    begin(4)
    go(first_hw[1] - 1, 0)
    layer(0, [None, (first_hw[0], 1), None, None])
    begin(5)
    copies = [
        pltpu.make_async_copy(pooled_hbm, kst, load_s.at[0]),
        pltpu.make_async_copy(chars_hbm, chars, load_s.at[3]),
    ]
    for copy in copies:
        copy.start()
    go(first_hw[1] + 3, 0)
    for copy in copies:
        copy.wait()

    dchars = kgt.at[:VROWS]
    dchars[...] = jnp.zeros((VROWS, words), f32)
    wgrad = knl.at[:, :TAPS]
    wgrad[...] = jnp.zeros((own, TAPS), f32)
    slots = [dpre.at[:own], dpre.at[own:], full.at[:own], full.at[own:]]

    def place_at(p, blocks, slot):
        window = pl.ds(p * CHAR_DIM if isinstance(p, int) else pl.multiple_of(p * CHAR_DIM, CHAR_DIM), TAPS)
        taps = chars[window, :]
        dconv = slots[slot]
        for block in range(blocks):
            rows = pl.ds(block * FBLOCK, FBLOCK)
            value = jnp.exp(dot(conv_ref[rows, :], taps, 1, 0) - kst[rows, :]) * gs[rows, :]
            if isinstance(p, int) and p >= limits[block][0]:
                value = jnp.where(lim_ref[rows, :][:, :1] >= p, value, 0.0)
            dconv[rows, :] = value.astype(bf16)
        rows = pl.ds(0, blocks * FBLOCK)
        wgrad[rows, :] += dot(dconv[rows, :], taps, 1, 1)
        dchars[window, :] += dot(conv_t_ref[:, : blocks * FBLOCK], dconv[rows, :], 1, 0)

    left = len(ticks)
    done = 0

    def spend(until):
        nonlocal done
        while done < until:
            call, *which = ticks.pop(0)
            call(*which)
            done += 1

    for q in range(4):
        arrive(0, q)

        def pooled_grad(c, carry, q=q):
            rows = quarter_rows(c, q)
            _, slope = gelu_both(kst[rows, :] + packed_ref[rows, taps_used : taps_used + 1])
            grad = gs[rows, :] * slope
            gs[rows, :] = grad
            pack[rows, :] += bias_lane(64, taps_used, jnp.sum(grad, axis=1, keepdims=True))
            return carry

        lax.fori_loop(0, quarter // 64, pooled_grad, 0)
    always = min(full_places for full_places, _ in limits)
    ever = max(some for _, some in limits)
    turns = always // 4
    stretches = 6
    for s in range(stretches):
        def four(i, carry):
            for u in range(4):
                place_at(i * 4 + u, len(limits), u)
            return carry

        lax.fori_loop(turns * s // stretches, turns * (s + 1) // stretches, four, 0)
        spend(left * (s + 1) // stretches)
    for p in range(turns * 4, ever):
        blocks = 1 + max(block for block, (_, some) in enumerate(limits) if p < some)
        place_at(p, blocks, p % 4)
    lane = lax.broadcasted_iota(jnp.int32, (own, TAPS), 1)
    keep = (lane < (CHARS - lim_ref[...]) * CHAR_DIM) & (lane < taps_used)
    result = (pack[...] + jnp.where(keep, wgrad[...], 0.0)).astype(bf16)
    convg[(slice(None),) * (depth + 2) + (slice(0, per),)] = result.reshape(
        (2,) * (depth + 2) + (per, LANE)
    )
    begin(6)

    ids_count = TABLE_ROWS // CHAR_DIM * LANE

    def spread(c, total):
        for i in range(5):
            rows = pl.ds(pl.multiple_of((c * 5 + i) * CHAR_DIM, CHAR_DIM), CHAR_DIM)
            row = pl.ds(c * 5 + i, 1)
            ids = jnp.concatenate([ids_ref[0, row, :], ids_ref[1, row, :]], axis=1)
            total = total + dot(dchars[rows, :].astype(bf16), onehot_chars(ids, ids_count), 1, 1)
        return total

    table = lax.fori_loop(0, CHARS // 5, spread, jnp.zeros((CHAR_DIM, ids_count), f32))
    for j in range(ids_count // LANE):
        vec_ref[j * CHAR_DIM : (j + 1) * CHAR_DIM, :] = table[:, j * LANE : (j + 1) * LANE]
    totals = Totals(place, vec_ref, inbox, total_s, total_r)
    for call, *which in ticks:
        call(*which)
    for i in range(len(totals.partners)):
        totals.start(i)
        if i < scatter.stages:
            for k in of_array[6]:
                scatter.add(k, i)
        totals.end(i)
    scatter.finish()


def embedder_backward(
    enc, de_low, base, proj_all, low, packed, conv, lim, ids, vec, kept, pooled, chars, lines, per,
    taps_used, ident,
):
    own, words = low.shape
    limits = tuple(block_limits(per, s, s + FBLOCK) for s in range(0, own, FBLOCK))
    shape = jax.ShapeDtypeStruct
    tall = max(per, 16)
    depth = (lines - 1).bit_length()
    lead = (2,) * (depth + 2)
    whole = []
    for a in enc:
        rows = -(-a.shape[1] // 16) * 16
        a = jnp.pad(a, ((0, 0), (0, rows - a.shape[1]), (0, 0)))
        whole.append(a.reshape(lead + a.shape[1:]))
    width = proj_all.shape[1]
    made = [
        shape(lead + (tall, width), bf16),
        shape(lead + (2 * per, FILTERS), bf16),
        shape(lead + (2 * per, FILTERS), bf16),
        shape(lead + (tall, LANE), bf16),
    ]
    arrays = whole + made
    pieces = cut(arrays, 48)
    near_first = [f"z{i}" for i in range(depth)]
    orders = [["y"] + near_first for array, _, _ in pieces]
    land, outs, bufs, sems = Scatter.shapes(arrays, pieces, depth)
    outs[4:6] = [shape((2,) + outs[4].shape, f32)]
    dma = pltpu.SemaphoreType.DMA
    vmem = pl.BlockSpec(memory_space=pltpu.VMEM)
    steps = 3 + (lines - 1).bit_length()
    layers = [
        (state, nonlin, gate, both, weight.reshape(lead + (2 * per, FILTERS)))
        for state, nonlin, gate, both, weight in kept
    ]
    result = pl.pallas_call(
        functools.partial(back_kernel, lines, limits, per, pieces, orders, taps_used),
        out_shape=tuple(land + [made[1], made[1]] + outs + [shape(vec.shape, f32)]),
        in_specs=[ANYWHERE] * 4 + [vmem] * 9 + [ANYWHERE] * 12,
        out_specs=tuple([ANYWHERE] * (len(land) + 2) + [vmem] * (len(outs) + 1)),
        scratch_shapes=bufs
        + sems
        + [
            pltpu.VMEM((own, words), f32), pltpu.VMEM((own, words), f32), pltpu.VMEM((own, words), f32),
            pltpu.VMEM((2 * own, words), bf16),
            pltpu.VMEM((2,) + lead[2:] + (2 * per, FILTERS), bf16),
            pltpu.VMEM((words, FILTERS), f32),
            pltpu.VMEM((2 * own, words), bf16), pltpu.VMEM((words, 2 * own), bf16),
            pltpu.VMEM((own, words), f32), pltpu.VMEM((words, width), bf16),
            pltpu.VMEM((own, words), bf16),
            pltpu.VMEM((2, own, words), bf16),
            pltpu.VMEM(made[0].shape, bf16), pltpu.VMEM(made[3].shape, bf16),
            pltpu.VMEM((own, LANE), f32), pltpu.VMEM((VROWS, words), bf16),
            pltpu.VMEM((steps,) + vec.shape, f32),
            dma((4,)), dma((2,)), dma((2,)), dma((3, 4)), dma((3, 4)), dma((steps,)), dma((steps,)),
        ],
        compiler_params=pltpu.CompilerParams(
            collective_id=ident, has_side_effects=True, vmem_limit_bytes=62 << 20
        ),
    )(
        *whole, de_low, base, proj_all, low, packed, conv, conv.T, lim, ids, vec,
        *layers[0], *layers[1], pooled, chars,
    )
    outs = result[len(land) + 2 : -1]
    heights = [a.shape[1] for a in enc] + [per, 2, per]
    return [o[:h] for o, h in zip(outs, heights)], result[-1]


def norm_forward(summed):
    centred = summed - jnp.mean(summed, axis=-1, keepdims=True)
    inv_std = lax.rsqrt(jnp.mean(centred * centred, axis=-1, keepdims=True) + norm_eps)
    return centred * inv_std, inv_std


def norm_backward(grad_out, normalized, inv_std, gain):
    grad_norm = grad_out * gain
    return inv_std * (
        grad_norm
        - jnp.mean(grad_norm, axis=-1, keepdims=True)
        - normalized * jnp.mean(grad_norm * normalized, axis=-1, keepdims=True)
    )


def split_two(x):
    high = x.astype(bf16)
    return high, (x - high.astype(f32)).astype(bf16)


def per_device(
    char_ids, mask_pos, out_grad, char_table, conv_weight, conv_bias, highway_weight, highway_bias,
    proj_weight, proj_bias, qkv_weight, qv_bias, out_weight, out_bias, ln1_gain, ln1_bias, up_weight,
    up_bias, down_weight, down_bias, ln2_gain, ln2_bias,
):
    side = lax.axis_index(PAIR)
    per = conv_weight.shape[1]
    ndp = FILTERS // (2 * per)
    rows_here = char_ids.shape[0]
    words = 2 * rows_here
    own = ndp * per
    layers = highway_weight.shape[0]
    ids_count = char_table.shape[0]
    padded_ids = -(-ids_count // 128) * 128

    taps_used = conv_weight.shape[0]
    packed = jnp.concatenate(
        [
            conv_weight.T.astype(f32),
            conv_bias[:, None].astype(f32),
            highway_bias.reshape(2 * layers, per).T.astype(f32),
            jnp.zeros((per, TAPS - taps_used - 1 - 2 * layers), f32),
        ],
        axis=1,
    )
    highway_t = highway_weight.transpose(0, 2, 3, 1)
    lines = ndp // 4
    blocks = [highway_t[i].reshape(2 * per, FILTERS) for i in range(layers)]
    filter_index = jnp.arange(own, dtype=jnp.int32)
    filter_index = (filter_index // per) * (2 * per) + side * per + filter_index % per
    filter_width = width_of(filter_index).astype(jnp.int32)
    lim = jnp.broadcast_to((CHARS - filter_width)[:, None], (own, 128))
    table_t = jnp.pad(char_table.T, ((0, 0), (0, padded_ids - ids_count)))
    (
        packed_all, first_all, second_all, proj_all, both_a, nonlin_a, gate_a, ids, chars, conv_all,
        pooled_raw, state, state_b, both_b, nonlin_b, gate_b, state_low, embedded,
    ) = embedder_forward(
        char_ids.T, table_t, lim, packed, blocks[0], blocks[1], proj_weight, proj_bias.astype(f32)[None],
        lines, per, taps_used, 1,
    )
    packed_all = packed_all.reshape(own, TAPS)
    proj_all = proj_all.reshape(own, D)
    kept = [
        (state, nonlin_a, gate_a, both_a, first_all), (state_b, nonlin_b, gate_b, both_b, second_all),
    ]

    emb_low = embedded.astype(bf16)
    seqs = words // LEN
    width = qkv_weight.shape[2]
    heads = width // HEAD_DIM
    qkv_t = qkv_weight.transpose(1, 0, 2)
    qkv_bias = jnp.stack([qv_bias[0], jnp.zeros_like(qv_bias[0]), qv_bias[1]]).astype(f32)
    projected = [
        (dot(emb_low, qkv_t[part], 1, 0) + qkv_bias[part][None]).astype(bf16) for part in range(3)
    ]

    def by_head(x):
        return x.reshape(-1, heads, HEAD_DIM).transpose(1, 0, 2)

    queries, keys, values = (by_head(part) for part in projected)
    scale = 1.0 / math.sqrt(HEAD_DIM)

    def probs_of(q):
        scores = jnp.einsum("hqd,hkd->hqk", q, keys, preferred_element_type=f32) * scale
        terms = jnp.exp(scores - jnp.max(scores, axis=-1, keepdims=True))
        return terms / jnp.sum(terms, axis=-1, keepdims=True)

    mixed = (
        jnp.einsum("hqk,hkd->qhd", probs_of(queries).astype(bf16), values, preferred_element_type=f32)
        .reshape(words, width)
        .astype(bf16)
    )
    att_part = dot(mixed, out_weight, 1, 0)
    gain_one, gain_two = ln1_gain.astype(f32), ln2_gain.astype(f32)
    summed = embedded + (
        att_part + pair_swap(att_part.astype(bf16)).astype(f32) + out_bias.astype(f32)
    )
    normalized_one, inv_std_one = norm_forward(summed)
    normed = normalized_one * gain_one + ln1_bias.astype(f32)
    normed_low = normed.astype(bf16)
    hidden = gelu(dot(normed_low, up_weight, 1, 0) + up_bias.astype(f32)).astype(bf16)
    ffn_part = dot(hidden, down_weight, 1, 0)

    slots = mask_pos.shape[1]
    padded_slots = -(-slots // 16) * 16
    positions = jnp.pad(mask_pos[0], (0, padded_slots - slots), constant_values=-1)
    pick = (positions[:, None] == jnp.arange(words, dtype=jnp.int32)[None, :]).astype(bf16)
    slot_grad = jnp.pad(out_grad[0], ((0, padded_slots - slots), (0, 0)))
    n1_high, n1_low = split_two(normalized_one)
    n1_s = dot(pick, n1_high, 1, 0) + dot(pick, n1_low, 1, 0)
    r1_s = jnp.sum(jnp.where(pick > 0, inv_std_one.T, 0.0), axis=1, keepdims=True)
    normed_s = n1_s * gain_one + ln1_bias.astype(f32)
    normed_low_s = dot(pick, normed_low, 1, 0).astype(bf16)
    mixed_s = dot(pick, mixed, 1, 0).astype(bf16)
    emb_s = dot(pick, emb_low, 1, 0).astype(bf16)
    queries_s = jnp.einsum("mw,hwd->hmd", pick, queries, preferred_element_type=f32).astype(bf16)
    hidden_pre_s = dot(normed_low_s, up_weight, 1, 0) + up_bias.astype(f32)
    hidden_s = gelu(hidden_pre_s).astype(bf16)
    ffn_s = dot(hidden_s, down_weight, 1, 0)

    theirs = lax.dynamic_slice_in_dim(ffn_part, (1 - side) * rows_here, rows_here, 0)
    got = pair_swap(jnp.concatenate([theirs, ffn_s], axis=0).astype(bf16)).astype(f32)
    start = side * rows_here
    second = (
        lax.dynamic_slice_in_dim(normed, start, rows_here, 0)
        + (lax.dynamic_slice_in_dim(ffn_part, start, rows_here, 0) + got[:rows_here])
        + down_bias.astype(f32)
    )
    normalized_two, _ = norm_forward(second)
    result = normalized_two * gain_two + ln2_bias.astype(f32)
    n2_s, r2_s = norm_forward(normed_s + (ffn_s + got[rows_here:]) + down_bias.astype(f32))

    grad_second = norm_backward(slot_grad, n2_s, r2_s, gain_two)
    ln2_gain_grad = jnp.sum(slot_grad * n2_s, axis=0)
    ln2_bias_grad = jnp.sum(slot_grad, axis=0)
    dffn = grad_second.astype(bf16)
    down_bias_grad = jnp.sum(dffn, axis=0, dtype=f32)
    down_grad_t = dot(dffn, hidden_s, 0, 0)
    dpre = (dot(dffn, down_weight, 1, 1) * gelu_both(hidden_pre_s)[1]).astype(bf16)
    up_bias_grad = jnp.sum(dpre, axis=0, dtype=f32)
    up_grad = dot(normed_low_s, dpre, 0, 0)
    dn_part = dot(dpre, up_weight, 1, 1)
    grad_normed = grad_second + (dn_part + pair_swap(dn_part.astype(bf16)).astype(f32))
    grad_first = norm_backward(grad_normed, n1_s, r1_s, gain_one)
    ln1_gain_grad = jnp.sum(grad_normed * n1_s, axis=0)
    ln1_bias_grad = jnp.sum(grad_normed, axis=0)
    dattn = grad_first.astype(bf16)
    out_bias_grad = jnp.sum(dattn, axis=0, dtype=f32)
    out_grad_t = dot(dattn, mixed_s, 0, 0)
    dmixed = by_head(dot(dattn, out_weight, 1, 1).astype(bf16))
    probs = probs_of(queries_s)
    dvalues = jnp.einsum("hqk,hqd->khd", probs.astype(bf16), dmixed, preferred_element_type=f32)
    dprobs = jnp.einsum("hqd,hkd->hqk", dmixed, values, preferred_element_type=f32)
    dscores = (probs * (dprobs - jnp.sum(probs * dprobs, axis=-1, keepdims=True))).astype(bf16)
    dqueries = jnp.einsum("hqk,hkd->qhd", dscores, keys, preferred_element_type=f32) * scale
    dkeys = jnp.einsum("hqk,hqd->khd", dscores, queries_s, preferred_element_type=f32) * scale
    dq = dqueries.reshape(padded_slots, width).astype(bf16)
    dk = dkeys.reshape(words, width).astype(bf16)
    dv = dvalues.reshape(words, width).astype(bf16)
    qv_bias_grad = jnp.stack([jnp.sum(dq, axis=0, dtype=f32), jnp.sum(dv, axis=0, dtype=f32)])
    qkvo_grad = [dot(emb_s, dq, 0, 0), dot(emb_low, dk, 0, 0), dot(emb_low, dv, 0, 0), out_grad_t]
    dq_high, dq_low = split_two(dot(dq, qkv_t[0], 1, 1))
    gf_high, gf_low = split_two(grad_first)
    back = dot(pick, jnp.concatenate([dq_high, gf_high], axis=1), 0, 0) + dot(
        pick, jnp.concatenate([dq_low, gf_low], axis=1), 0, 0
    )
    de_part = back[:, :D] + dot(dk, qkv_t[1], 1, 1) + dot(dv, qkv_t[2], 1, 1)
    encoder_grads = [
        g.astype(bf16).reshape(ndp, D // ndp, -1)
        for g in (up_grad, down_grad_t, jnp.concatenate(qkvo_grad, axis=1))
    ]
    first = side == 0
    shared = [
        jnp.where(first, g, 0.0)
        for g in (
            out_bias_grad, ln1_gain_grad, ln1_bias_grad, down_bias_grad, ln2_gain_grad, ln2_bias_grad,
        )
    ]
    own_side = jnp.concatenate([qv_bias_grad.reshape(-1), up_bias_grad])
    flat = jnp.concatenate([*shared, jnp.where(first, own_side, 0.0), jnp.where(first, 0.0, own_side)])
    rows_flat = -(-flat.shape[0] // 1024) * 8
    flat = jnp.pad(flat, (HEAD_ROWS * LANE, rows_flat * LANE - flat.shape[0])).reshape(-1, LANE)

    (up_mine, down_mine, qkvo_mine, proj_mine, highway_mine, conv_mine), flat = embedder_backward(
        encoder_grads, de_part.astype(bf16), back[:, D:] + de_part, proj_all, state_low, packed_all,
        conv_all, lim, ids, flat, kept, pooled_raw, chars, lines, per, taps_used, 3,
    )
    table_grad_t = flat[:TABLE_ROWS].reshape(-1, CHAR_DIM, LANE).transpose(1, 0, 2).reshape(CHAR_DIM, -1)
    flat = flat[TABLE_ROWS:].reshape(-1)
    proj_bias_grad = flat[:D]
    flat = flat[(HEAD_ROWS - TABLE_ROWS) * LANE :]
    out_bias_grad, ln1_gain_grad, ln1_bias_grad, down_bias_grad, ln2_gain_grad, ln2_bias_grad = (
        flat[i * D : (i + 1) * D] for i in range(6)
    )
    at = 6 * D
    size = own_side.shape[0]
    own_side = jnp.where(first, flat[at : at + size], flat[at + size : at + 2 * size])
    qv_bias_grad = own_side[: 2 * width].reshape(2, width)
    up_bias_grad = own_side[2 * width :]
    conv_bias_mine = conv_mine[:, taps_used]
    highway_bias_mine = [
        conv_mine[:, taps_used + 1 + 2 * i : taps_used + 3 + 2 * i].T for i in range(layers)
    ]
    conv_mine = conv_mine[:, :taps_used]
    qkv_mine = jnp.stack([qkvo_mine[:, i * width : (i + 1) * width] for i in range(3)])
    out_mine = qkvo_mine[:, 3 * width :]
    highway_mine = highway_mine.reshape(layers, 2, per, FILTERS).transpose(0, 3, 1, 2)
    highway_bias_mine = jnp.stack(highway_bias_mine).reshape(layers, 2, per)
    return (
        result.astype(bf16),
        table_grad_t.T[:ids_count],
        conv_mine.T,
        conv_bias_mine,
        highway_mine,
        highway_bias_mine,
        proj_mine,
        proj_bias_grad,
        qkv_mine.transpose(1, 0, 2),
        qv_bias_grad,
        out_mine.T,
        out_bias_grad,
        ln1_gain_grad,
        ln1_bias_grad,
        up_mine,
        up_bias_grad,
        down_mine.T,
        down_bias_grad,
        ln2_gain_grad,
        ln2_bias_grad,
    )


def solution(mesh):
    placed = (
        P(("dp", "tensor"), None),
        P("dp", None),
        P("dp", None, None),
        P(),
        P(None, ("dp", "tensor")),
        P(("dp", "tensor")),
        P(None, None, None, ("dp", "tensor")),
        P(None, None, ("dp", "tensor")),
        P(("dp", "tensor"), None),
        P(),
        P(None, None, "tensor"),
        P(None, "tensor"),
        P("tensor", None),
        P(),
        P(),
        P(),
        P(None, "tensor"),
        P("tensor"),
        P("tensor", None),
        P(),
        P(),
        P(),
    )
    return jax.shard_map(
        per_device,
        mesh=mesh,
        in_specs=placed,
        out_specs=(
            P(("dp", "tensor"), None),
            P(),
            P(None, ("dp", "tensor")),
            P(("dp", "tensor")),
            P(None, None, None, ("dp", "tensor")),
            P(None, None, ("dp", "tensor")),
            P(("dp", "tensor"), None),
            P(),
            P("dp", None, "tensor"),
            P(None, "tensor"),
            P("tensor", "dp"),
            P(),
            P(),
            P(),
            P("dp", "tensor"),
            P("tensor"),
            P("tensor", "dp"),
            P(),
            P(),
            P(),
        ),
        check_vma=False,
    )
```
